32 devices in a mesh: gx: 8 (over z, x), gy: 4 (over y, core).
Axes of the slice: x: 2, y: 2, z: 4, core: 2. Of those that a mesh axis runs over, the one named last changes fastest.
Arguments:
- load: float32 [128, 64, 512], P('gx', 'gy'), may hold values from -130 to 130
- conductivity: bfloat16 [128, 64, 512], P('gx', 'gy'), may hold values from 0.29882812 to 3
- flags: int32 [128, 64, 512], P('gx', 'gy'), may hold values from 0 to 1, as said below
- region: int32 [16, 8, 64], P('gx', 'gy'), may hold values from 0 to 2
- kappa_table: float32 [3], replicated, may hold values from 10 to 100
Outputs:
- solution: float32 [128, 64, 512], P('gx', 'gy')
- residual: float32 [128, 64, 512], P('gx', 'gy')
- direction: float32 [128, 64, 512], P('gx', 'gy')
The draws below stay inside these ranges and needn't reach their ends.
Inputs may be any that keep to these rules, and one draw needn't show every extreme that they name: flags are 1 only at nodes of the first layer along the third dimension, and all copies of one shared node carry the same flag.
All inputs are finite; a program needn't handle non-finite values.
Results may differ from the reference program's by a relative error of at most 0.0003.
Values sent between devices are 32-bit elements; how exact they have to be, the bound alone decides.
A program may use at most 64 MiB of HBM per device.

```python
import math
import jax
import jax.numpy as jnp
import numpy as np
from jax import lax

NREG = 3
EZ = 64
EXT = 16
EYT = 8
NX = 128
NY = 64
NZ = 512


def draw_load(key, part):
    key_base, key_plane = jax.random.split(key)
    pos_x = jnp.arange(NX, dtype=jnp.float32) / NX
    pos_y = jnp.arange(NY, dtype=jnp.float32) / NY
    amplitude = (1.0 + pos_x)[:, None, None] * (1.0 + pos_y)[None, :, None]
    plane_scale = jnp.exp(jax.random.uniform(key_plane, (NZ,), jnp.float32, 0.0, math.log(10.0)))
    base_values = jnp.clip(jax.random.normal(key_base, (NX, NY, NZ), jnp.float32), -3.0, 3.0)
    return (base_values * amplitude * plane_scale[None, None, :]).astype(jnp.float32)


def draw_flags(key, part):
    phys_nx = 7 * (NX // 8) + 1
    phys_ny = 7 * (NY // 8) + 1
    random_bits = jax.random.randint(key, (phys_nx, phys_ny), 0, 2, dtype=jnp.int32)
    rows_x = jnp.arange(NX, dtype=jnp.int32)
    rows_y = jnp.arange(NY, dtype=jnp.int32)
    phys_x = rows_x // 8 * 7 + rows_x % 8
    phys_y = rows_y // 8 * 7 + rows_y % 8
    plane_bits = random_bits[phys_x][:, phys_y]
    layer_ids = jnp.arange(NZ, dtype=jnp.int32)
    return jnp.where(layer_ids[None, None, :] == 0, plane_bits[:, :, None], 0).astype(jnp.int32)


def set_ends(values, rng, smallest, largest):
    place = [jax.random.randint(jax.random.fold_in(rng, axis), (), 0, length) for axis, length in enumerate(values.shape)]
    longest = values.shape.index(max(values.shape))
    neighbour = place[:longest] + [(place[longest] + 1) % values.shape[longest]] + place[longest + 1:]
    return values.at[tuple(place)].set(smallest).at[tuple(neighbour)].set(largest)


def shard_levels(key, shape, cuts, smallest, largest):
    factor_of = 1.0
    for dim, shards_of in cuts:
        draws = jax.random.uniform(jax.random.fold_in(jax.random.fold_in(key, 6), dim), (shards_of,), jnp.float32, smallest / len(cuts), largest / len(cuts))
        factor_of = factor_of * jnp.repeat(jnp.exp(draws), shape[dim] // shards_of).reshape((-1,) + (1,) * (len(shape) - 1 - dim))
    return factor_of


def setup_inputs(seed: int = 0) -> dict:
    streams_of = jax.random.split(jax.random.key(seed), 6)
    return {
        "load": draw_load(jax.random.fold_in(streams_of[5], 71), 0),
        "conductivity": jnp.clip(jnp.exp(math.log(3.0) - 2.306499 * jax.random.uniform(streams_of[1], (NX, NY, NZ), jnp.float32) ** shard_levels(streams_of[1], (NX, NY, NZ), ((0, 8), (1, 4)), -0.2, 0.2)), 0.29882812, 3.0).astype(jnp.bfloat16),
        "flags": draw_flags(jax.random.fold_in(streams_of[5], 71), 0),
        "region": set_ends(jax.random.randint(streams_of[3], (EXT, EYT, EZ), 0, NREG), jax.random.fold_in(streams_of[3], 1), 0, NREG - 1).astype(jnp.int32),
        "kappa_table": jnp.clip(jnp.exp(jax.random.uniform(streams_of[4], (NREG,), jnp.float32, math.log(10.0), math.log(100.0))), 10.0, 100.0),
    }


CHEB_CENTER = 24.0
CHEB_HALF = 23.0


def gll_tables():
    nodes_gll = np.array([-1.0, -0.8717401485096066, -0.5917001814331423, -0.2092992179024789, 0.2092992179024789, 0.5917001814331423, 0.8717401485096066, 1.0])
    legendre_prev = np.ones(8)
    legendre_now = nodes_gll.copy()
    for degree in range(1, 7):
        legendre_next = ((2 * degree + 1) * nodes_gll * legendre_now - degree * legendre_prev) / (degree + 1)
        legendre_prev = legendre_now
        legendre_now = legendre_next
    weights_gll = 2.0 / (56.0 * legendre_now ** 2)
    diff_table = np.zeros((8, 8))
    for row_index in range(8):
        for col_index in range(8):
            if row_index != col_index:
                diff_table[row_index, col_index] = legendre_now[row_index] / (legendre_now[col_index] * (nodes_gll[row_index] - nodes_gll[col_index]))
    diff_table[0, 0] = -14.0
    diff_table[7, 7] = 14.0
    return diff_table, weights_gll


def pair_fold(padded, which_dim):
    length = padded.shape[which_dim]
    blocks = (length - 2) // 8
    lower_rows = lax.slice_in_dim(padded, 0, length, 8, which_dim)
    upper_rows = lax.slice_in_dim(padded, 1, length, 8, which_dim)
    joined = lower_rows + upper_rows
    inner_rows = lax.slice_in_dim(padded, 1, length - 1, 1, which_dim)
    inner_rows = inner_rows.reshape(inner_rows.shape[:which_dim] + (blocks, 8) + inner_rows.shape[which_dim + 1:])
    first_rows = jnp.expand_dims(lax.slice_in_dim(joined, 0, blocks, 1, which_dim), which_dim + 1)
    last_rows = jnp.expand_dims(lax.slice_in_dim(joined, 1, blocks + 1, 1, which_dim), which_dim + 1)
    middle = lax.slice_in_dim(inner_rows, 1, 7, 1, which_dim + 1)
    result = jnp.concatenate([first_rows, middle, last_rows], axis=which_dim + 1)
    return result.reshape(inner_rows.shape[:which_dim] + (blocks * 8,) + inner_rows.shape[which_dim + 2:])


def apply_local(vector, coefficient, reaction, derivative, block_deriv):
    rows_x, rows_y, rows_z = vector.shape
    block_z = block_deriv.shape[0]
    highest = lax.Precision.HIGHEST
    shape_x = (rows_x // 8, 8, rows_y, rows_z)
    grad_x = jnp.einsum('ab,ebyz->eayz', derivative, vector.reshape(shape_x), precision=highest)
    back_x = jnp.einsum('ab,eayz->ebyz', derivative, grad_x * coefficient.reshape(shape_x), precision=highest)
    shape_y = (rows_x, rows_y // 8, 8, rows_z)
    grad_y = jnp.einsum('ab,xebz->xeaz', derivative, vector.reshape(shape_y), precision=highest)
    back_y = jnp.einsum('ab,xeaz->xebz', derivative, grad_y * coefficient.reshape(shape_y), precision=highest)
    shape_z = (rows_x, rows_y, rows_z // block_z, block_z)
    grad_z = jnp.einsum('xykb,ab->xyka', vector.reshape(shape_z), block_deriv, precision=highest)
    back_z = jnp.einsum('xyka,ab->xykb', grad_z * coefficient.reshape(shape_z), block_deriv, precision=highest)
    return back_x.reshape(vector.shape) + back_y.reshape(vector.shape) + back_z.reshape(vector.shape) + reaction * vector


def diag_local(coefficient, reaction, derivative, block_deriv):
    rows_x, rows_y, rows_z = coefficient.shape
    block_z = block_deriv.shape[0]
    highest = lax.Precision.HIGHEST
    square_d = derivative * derivative
    square_block = block_deriv * block_deriv
    part_x = jnp.einsum('qa,eqyz->eayz', square_d, coefficient.reshape(rows_x // 8, 8, rows_y, rows_z), precision=highest)
    part_y = jnp.einsum('qa,xeqz->xeaz', square_d, coefficient.reshape(rows_x, rows_y // 8, 8, rows_z), precision=highest)
    part_z = jnp.einsum('xykq,qa->xyka', coefficient.reshape(rows_x, rows_y, rows_z // block_z, block_z), square_block, precision=highest)
    return part_x.reshape(coefficient.shape) + part_y.reshape(coefficient.shape) + part_z.reshape(coefficient.shape) + reaction


def share_weights(count, offset, total):
    position = offset + jnp.arange(count, dtype=jnp.int32)
    within = position % 8
    shared = ((within == 7) & (position != total - 1)) | ((within == 0) & (position != 0))
    return jnp.where(shared, 0.5, 1.0).astype(jnp.float32)


def precondition(residual_in, diagonal, operator):
    update = residual_in / (CHEB_CENTER * diagonal)
    approx = update
    rho_prev = CHEB_HALF / CHEB_CENTER
    for sweep_index in range(2):
        rho_next = 1.0 / (2.0 * CHEB_CENTER / CHEB_HALF - rho_prev)
        update = rho_next * rho_prev * update + (2.0 * rho_next / CHEB_HALF) * (residual_in - operator(approx)) / diagonal
        approx = approx + update
        rho_prev = rho_next
    return approx


def node_kappa(region, kappa_table):
    element_kappa = jnp.zeros(region.shape, jnp.float32)
    for region_id in range(NREG):
        element_kappa = element_kappa + (region == region_id).astype(jnp.float32) * kappa_table[region_id]
    return jnp.repeat(jnp.repeat(jnp.repeat(element_kappa, 8, axis=0), 8, axis=1), 8, axis=2)


def assemble_global(vector):
    padded = jnp.pad(vector, 1)
    return pair_fold(pair_fold(pair_fold(padded, 0), 1), 2)


def reference(load, conductivity, flags, region, kappa_table):
    diff_np, weights_np = gll_tables()
    derivative = jnp.asarray(diff_np, dtype=jnp.float32)
    gll_weights = jnp.asarray(weights_np, dtype=jnp.float32)
    weight_x = jnp.tile(gll_weights, NX // 8)
    weight_y = jnp.tile(gll_weights, NY // 8)
    weight_z = jnp.tile(gll_weights, NZ // 8)
    quad_weights = weight_x[:, None, None] * weight_y[None, :, None] * weight_z[None, None, :]
    coefficient = quad_weights * conductivity.astype(jnp.float32)
    reaction = quad_weights * node_kappa(region, kappa_table)
    keep_mask = (1 - flags).astype(jnp.float32)
    mult_weights = share_weights(NX, 0, NX)[:, None, None] * share_weights(NY, 0, NY)[None, :, None] * share_weights(NZ, 0, NZ)[None, None, :]

    def operator(vector):
        local_out = apply_local(keep_mask * vector, coefficient, reaction, derivative, derivative)
        return keep_mask * assemble_global(local_out) + (1.0 - keep_mask) * vector

    diagonal = keep_mask * assemble_global(diag_local(coefficient, reaction, derivative, derivative)) + (1.0 - keep_mask)
    first_res = keep_mask * assemble_global(load)
    first_z = precondition(first_res, diagonal, operator)
    image_vec = operator(first_z)
    first_dot = jnp.sum(first_res * first_z * mult_weights)
    curv_dot = jnp.sum(first_z * image_vec * mult_weights)
    step_length = first_dot / curv_dot
    solution = step_length * first_z
    residual = first_res - step_length * image_vec
    next_z = precondition(residual, diagonal, operator)
    next_dot = jnp.sum(residual * next_z * mult_weights)
    direction = next_z + (next_dot / first_dot) * first_z
    return solution, residual, direction
```

```python
import functools

import jax
import jax.numpy as jnp
import numpy as np
from jax import lax
from jax.experimental import pallas as pl
from jax.experimental.pallas import tpu as pltpu
from jax.sharding import PartitionSpec as P

NREG = 3
CENTER = 24.0
HALF = 23.0
RHO0 = HALF / CENTER
RHO1 = 1.0 / (2.0 * CENTER / HALF - RHO0)
RHO2 = 1.0 / (2.0 * CENTER / HALF - RHO1)
C1, E1 = RHO1 * RHO0, 2.0 * RHO1 / HALF
C2, E2 = RHO2 * RHO1, 2.0 * RHO2 / HALF
MESH = pl.DeviceIdType.MESH
F32, BF16 = jnp.float32, jnp.bfloat16
DIRS = ((-1, 0), (1, 0), (0, -1), (0, 1), (-1, -1), (-1, 1), (1, -1), (1, 1))
OPP = (1, 0, 3, 2, 7, 6, 5, 4)
ROUNDS = 7


def gll_tables():
    nodes = np.array(
        [
            -1.0,
            -0.8717401485096066,
            -0.5917001814331423,
            -0.2092992179024789,
            0.2092992179024789,
            0.5917001814331423,
            0.8717401485096066,
            1.0,
        ]
    )
    prev, now = np.ones(8), nodes.copy()
    for degree in range(1, 7):
        prev, now = now, ((2 * degree + 1) * nodes * now - degree * prev) / (degree + 1)
    weights = 2.0 / (56.0 * now**2)
    diff = np.zeros((8, 8))
    for a in range(8):
        for b in range(8):
            if a != b:
                diff[a, b] = now[a] / (now[b] * (nodes[a] - nodes[b]))
    diff[0, 0], diff[7, 7] = -14.0, 14.0
    return diff.astype(np.float32), weights.astype(np.float32)


def tables(rows_x, rows_y):
    d, w = gll_tables()
    mx = np.kron(np.kron(np.eye(rows_x // 8), d), np.eye(rows_y))
    my = np.kron(np.eye(rows_x * rows_y // 8), d)
    mz = np.kron(np.eye(32), d)
    fwd = np.concatenate([mx, my], 0)
    back = np.concatenate([mx.T, my.T], 1)
    dxy = (mx * mx).T + (my * my).T
    mats = [m.astype(np.float32) for m in (fwd, back, mz.T, mz, dxy, mz * mz)]
    wx, wy, wz = np.tile(w, rows_x // 8), np.tile(w, rows_y // 8), np.tile(w, 16)
    quad = (wx[:, None, None] * wy[None, :, None]) * wz[None, None, :]
    return *mats, quad.reshape(rows_x * rows_y, 128)


def split(v):
    hi = v.astype(BF16)
    return hi, (v - hi.astype(F32)).astype(BF16)


def dot(a, b):
    return jnp.dot(a, b, preferred_element_type=F32)


def left3(m, parts):
    hi, lo = parts
    return dot(m[0], hi) + dot(m[0], lo) + dot(m[1], hi)


def right3(parts, m):
    hi, lo = parts
    return dot(hi, m[0]) + dot(lo, m[0]) + dot(hi, m[1])


def sum_z(tiles):
    n = len(tiles)
    lane = lax.broadcasted_iota(jnp.int32, tiles[0].shape, 1)
    ups = [pltpu.roll(w, 127, 1) for w in tiles]
    downs = [pltpu.roll(w, 1, 1) for w in tiles]
    out = []
    for t, w in enumerate(tiles):
        zero = jnp.zeros_like(w)
        up = jnp.where(lane == 127, ups[t + 1] if t + 1 < n else zero, ups[t])
        down = jnp.where(lane == 0, downs[t - 1] if t > 0 else zero, downs[t])
        out.append(w + jnp.where(lane % 8 == 7, up, jnp.where(lane % 8 == 0, down, zero)))
    return out


def sum_rows(face):
    row = lax.broadcasted_iota(jnp.int32, face.shape, 0)
    up, down = pltpu.roll(face, 15, 0), pltpu.roll(face, 1, 0)
    zero = jnp.zeros_like(face)
    return face + jnp.where(row == 7, up, jnp.where(row == 8, down, zero))


def kernel(
    nx,
    ny,
    load_h,
    cond_h,
    flag_h,
    kz,
    fwd_f,
    back_f,
    zfwd_f,
    zback_f,
    dxy_f,
    dz_f,
    quad,
    sol_o,
    res_o,
    dir_o,
    fwd,
    back,
    zfwd,
    zback,
    dxy,
    dz,
    cond,
    flag,
    wbuf,
    wbuf2,
    coef,
    reac,
    keep,
    dinv,
    mrow,
    rvec,
    uvec,
    vec,
    r0,
    z0,
    sx,
    sy,
    sc,
    rx,
    ry,
    rc,
    part,
    part2,
    arx,
    ary,
    in_sem,
    send_sem,
    recv_sem,
    ax_send,
    ax_recv,
    ay_send,
    ay_recv,
):
    mx, my = lax.axis_index("gx"), lax.axis_index("gy")
    rows = 256
    nt = wbuf.shape[0]

    copies = [
        pltpu.make_async_copy(
            load_h.at[:, pl.ds(128 * t, 128)], wbuf.at[t], in_sem.at[t]
        )
        for t in range(nt)
    ]
    copies.append(pltpu.make_async_copy(cond_h, cond, in_sem.at[nt]))
    copies.append(pltpu.make_async_copy(flag_h.at[:, pl.ds(0, 128)], flag, in_sem.at[nt + 1]))
    for c in copies:
        c.start()

    rx[...] = jnp.zeros_like(rx)
    ry[...] = jnp.zeros_like(ry)
    rc[...] = jnp.zeros_like(rc)

    def inside(dx, dy):
        ok = None
        for d, m, n in ((dx, mx, nx), (dy, my, ny)):
            if d:
                c = m > 0 if d < 0 else m < n - 1
                ok = c if ok is None else jnp.logical_and(ok, c)
        return ok

    pairs = ((dxy_f, dxy), (dz_f, dz), (fwd_f, fwd), (back_f, back), (zfwd_f, zfwd), (zback_f, zback))
    for src, dst in pairs:
        dst[0], dst[1] = split(src[...])

    barrier = pltpu.get_barrier_semaphore()
    for d in range(1, nx):
        pl.semaphore_signal(
            barrier, inc=1, device_id=((mx + d) % nx, my), device_id_type=MESH
        )
    for d in range(1, ny):
        pl.semaphore_signal(
            barrier, inc=1, device_id=(mx, (my + d) % ny), device_id_type=MESH
        )
    for dx, dy in DIRS[4:]:

        @pl.when(inside(dx, dy))
        def _():
            pl.semaphore_signal(
                barrier, inc=1, device_id=(mx + dx, my + dy), device_id_type=MESH
            )

    peers = jnp.int32(nx - 1 + ny - 1)
    for dx, dy in DIRS[4:]:
        peers = peers + inside(dx, dy).astype(jnp.int32)
    pl.semaphore_wait(barrier, peers)

    def ends(k, i):
        if i < 2:
            return sx.at[k, i], rx.at[k, OPP[i]], rx.at[k, i]
        if i < 4:
            return sy.at[k, i - 2], ry.at[k, OPP[i] - 2], ry.at[k, i - 2]
        return sc.at[k, i - 4], rc.at[k, OPP[i] - 4], rc.at[k, i - 4]

    def start(k, w):
        for side, row in ((0, 0), (1, rows - 16)):
            tiles = sum_z([w[t, row : row + 16, :] for t in range(nt)])
            for t in range(nt):
                face = sum_rows(tiles[t])
                sx[k, side, t] = face
                sc[k, 2 * side, t : t + 1, :] = face[0:1, :]
                sc[k, 2 * side + 1, t : t + 1, :] = face[15:16, :]
        for side, row in ((0, 0), (1, 15)):
            tiles = sum_z([w[t, pl.ds(row, 16, stride=16), :] for t in range(nt)])
            for t in range(nt):
                sy[k, side, t] = sum_rows(tiles[t])
        for i, (dx, dy) in enumerate(DIRS):

            @pl.when(inside(dx, dy))
            def _():
                src, dst, _ = ends(k, i)
                pltpu.make_async_remote_copy(
                    src_ref=src,
                    dst_ref=dst,
                    send_sem=send_sem.at[k, i],
                    recv_sem=recv_sem.at[k, OPP[i]],
                    device_id=(mx + dx, my + dy),
                    device_id_type=MESH,
                ).start()

    def inner(w):
        for b in range(0, rows, 32):
            tiles = sum_z([w[t, b : b + 32, :] for t in range(nt)])
            for t in range(nt):
                w[t, b : b + 32, :] = tiles[t]
        for t in range(nt):
            s = w[t, 112:128, :] + w[t, 128:144, :]
            w[t, 112:128, :] = s
            w[t, 128:144, :] = s
            s = w[t, pl.ds(7, 16, stride=16), :] + w[t, pl.ds(8, 16, stride=16), :]
            w[t, pl.ds(7, 16, stride=16), :] = s
            w[t, pl.ds(8, 16, stride=16), :] = s

    def finish(k, w):
        for i, (dx, dy) in enumerate(DIRS):

            @pl.when(inside(dx, dy))
            def _():
                src, _, dst = ends(k, i)
                c = pltpu.make_async_remote_copy(
                    src_ref=src,
                    dst_ref=dst,
                    send_sem=send_sem.at[k, i],
                    recv_sem=recv_sem.at[k, i],
                    device_id=(mx + dx, my + dy),
                    device_id_type=MESH,
                )
                c.wait_recv()
                c.wait_send()

        for t in range(nt):
            w[t, 0:16, :] += rx[k, 0, t]
            w[t, rows - 16 : rows, :] += rx[k, 1, t]
            w[t, pl.ds(0, 16, stride=16), :] += ry[k, 0, t]
            w[t, pl.ds(15, 16, stride=16), :] += ry[k, 1, t]
            for c, row in enumerate((0, 15, rows - 16, rows - 1)):
                w[t, row : row + 1, :] += rc[k, c, t : t + 1, :]

    for c in copies[:nt]:
        c.wait()
    start(0, wbuf)
    copies[nt].wait()
    copies[nt + 1].wait()
    for t in range(nt):
        coef[t] = quad[...] * cond[:, 128 * t : 128 * (t + 1)].astype(F32)
        kt = kz[:, 128 * t : 128 * (t + 1)]
        kap = jnp.concatenate([kt[0:16]] * 8 + [kt[16:32]] * 8, 0)
        reac[t] = quad[...] * kap
    lane = lax.broadcasted_iota(jnp.int32, (rows, 128), 1)
    keep[...] = jnp.where(lane == 0, (1 - flag[...]).astype(F32), 1.0)

    for c in range(nt // 2):
        cc = jnp.concatenate([coef[2 * c], coef[2 * c + 1]], 1)
        parts = split(cc)
        out = left3(dxy, parts) + right3(parts, dz)
        for h in range(2):
            t = 2 * c + h
            wbuf2[t] = out[:, 128 * h : 128 * (h + 1)] + reac[t]
    start(1, wbuf2)

    row = lax.broadcasted_iota(jnp.int32, (rows, 128), 0)
    px, py = mx * 16 + (row >> 4), my * 16 + (row & 15)
    share = jnp.ones((rows, 128), F32)
    for p, total in ((px, 16 * nx), (py, 16 * ny)):
        shared = ((p & 7) == 7) & (p != total - 1) | ((p & 7) == 0) & (p != 0)
        share = share * jnp.where(shared, 0.5, 1.0)
    mrow[...] = share
    part[...] = jnp.zeros_like(part)

    def lane_share(t):
        z = lax.broadcasted_iota(jnp.int32, (8, 128), 1) + 128 * t
        shared = ((z & 7) == 7) & (z != 128 * nt - 1) | ((z & 7) == 0) & (z != 0)
        return jnp.where(shared, 0.5, 1.0)

    def add_part(slot, t, prod):
        s = jnp.sum((prod * mrow[...]).reshape(rows // 8, 8, 128), axis=0)
        part[8 * slot : 8 * slot + 8, :] += s * lane_share(t)

    inner(wbuf)
    inner(wbuf2)
    finish(0, wbuf)
    finish(1, wbuf2)
    for t in range(nt):
        res, dia = wbuf[t], wbuf2[t]
        if t == 0:
            res = keep[...] * res
            dia = keep[...] * dia + (1.0 - keep[...])
        inv = 1.0 / dia
        r0[t] = res
        dinv[t] = inv
        vec[t] = res * inv * (1.0 / CENTER)

    def apply(k):
        for c in range(nt // 2):
            first = vec[2 * c]
            if c == 0:
                first = keep[...] * first
            v = jnp.concatenate([first, vec[2 * c + 1]], 1)
            cc = jnp.concatenate([coef[2 * c], coef[2 * c + 1]], 1)
            rr = jnp.concatenate([reac[2 * c], reac[2 * c + 1]], 1)
            parts = split(v)
            gxy = left3(fwd, parts)
            gz = right3(parts, zfwd)
            fxy = split(gxy * jnp.concatenate([cc, cc], 0))
            fz = split(gz * cc)
            out = left3(back, fxy) + right3(fz, zback) + rr * v
            wbuf[2 * c] = out[:, :128]
            wbuf[2 * c + 1] = out[:, 128:]
        start(k, wbuf)
        inner(wbuf)

    def image_of(t):
        out = wbuf[t]
        if t == 0:
            out = keep[...] * out + (1.0 - keep[...]) * vec[t]
        return out

    def reduce_copy(src, dst, sems, slot, dev):
        return pltpu.make_async_remote_copy(
            src_ref=src,
            dst_ref=dst,
            send_sem=sems[0].at[slot[0]],
            recv_sem=sems[1].at[slot[1]],
            device_id=dev,
            device_id_type=MESH,
        )

    apply(2)
    finish(2, wbuf)
    for t in range(nt):
        u = C1 * vec[t] + E1 * (r0[t] - image_of(t)) * dinv[t]
        uvec[t] = u
        vec[t] = vec[t] + u
    apply(3)
    finish(3, wbuf)
    for t in range(nt):
        u = C2 * uvec[t] + E2 * (r0[t] - image_of(t)) * dinv[t]
        z = vec[t] + u
        vec[t] = z
        z0[t] = z
        add_part(0, t, r0[t] * z)
    apply(4)
    finish(4, wbuf)
    for t in range(nt):
        im = image_of(t)
        rvec[t] = im
        add_part(1, t, im * vec[t])
        vec[t] = im * dinv[t] * (1.0 / CENTER)
    apply(5)
    finish(5, wbuf)
    for t in range(nt):
        a0, im, az = vec[t], rvec[t], image_of(t)
        u = C1 * a0 + E1 * (im - az) * dinv[t]
        a1 = a0 + u
        uvec[t] = u
        vec[t] = a1
        add_part(
            2,
            t,
            im * ((1.0 + C2) * a1 + (E2 * CENTER - C2) * a0) - (CENTER * E2) * (az * a1),
        )
    arx[mx] = part[...]
    for d in range(1, nx):
        to = (mx + d) % nx
        reduce_copy(part, arx.at[mx], (ax_send, ax_recv), (d, mx), (to, my)).start()
    apply(6)
    for d in range(1, nx):
        frm = (mx + nx - d) % nx
        c = reduce_copy(part, arx.at[frm], (ax_send, ax_recv), (d, frm), (frm, my))
        c.wait_recv()
        c.wait_send()
    total = arx[0]
    for d in range(1, nx):
        total = total + arx[d]
    part2[...] = total
    ary[my] = total
    for d in range(1, ny):
        to = (my + d) % ny
        reduce_copy(part2, ary.at[my], (ay_send, ay_recv), (d, my), (mx, to)).start()
    finish(6, wbuf)
    for d in range(1, ny):
        frm = (my + ny - d) % ny
        c = reduce_copy(part2, ary.at[frm], (ay_send, ay_recv), (d, frm), (mx, frm))
        c.wait_recv()
        c.wait_send()
    total = ary[0]
    for d in range(1, ny):
        total = total + ary[d]

    def whole(slot):
        return jnp.sum(total[8 * slot : 8 * slot + 8], axis=(0, 1), keepdims=True)

    first, curv, quadratic = whole(0), whole(1), whole(2)
    step = first / curv
    second = step * step * quadratic - first
    beta1 = 1.0 + second / first
    for t in range(nt):
        q = vec[t] + C2 * uvec[t] + E2 * (rvec[t] - image_of(t)) * dinv[t]
        cols = slice(128 * t, 128 * (t + 1))
        sol_o[:, cols] = step * z0[t]
        res_o[:, cols] = r0[t] - step * rvec[t]
        dir_o[:, cols] = beta1 * z0[t] - step * q


def per_device(nx, ny, load, conductivity, flags, region, kappa_table):
    rows_x, rows_y, rows_z = load.shape
    rows, nt = rows_x * rows_y, rows_z // 128
    consts = [jnp.asarray(c) for c in tables(rows_x, rows_y)]
    ek = jnp.zeros(region.shape, F32)
    for region_id in range(NREG):
        ek = ek + (region == region_id).astype(F32) * kappa_table[region_id]
    kz = jnp.broadcast_to(
        jnp.repeat(ek, 8, axis=2)[:, :, None, :], (rows_x // 8, rows_y // 8, 8, rows_z)
    ).reshape(rows_x // 8 * rows_y, rows_z)
    big = pltpu.VMEM((nt, rows, 128), F32)
    face = pltpu.VMEM((ROUNDS, 2, nt, 16, 128), F32)
    line = pltpu.VMEM((ROUNDS, 4, 8, 128), F32)
    vm = pl.BlockSpec(memory_space=pltpu.VMEM)
    hbm = pl.BlockSpec(memory_space=pl.ANY)
    out = jax.ShapeDtypeStruct((rows, rows_z), F32)
    dma = pltpu.SemaphoreType.DMA
    outs = pl.pallas_call(
        functools.partial(kernel, nx, ny),
        out_shape=(out, out, out),
        in_specs=[hbm] * 3 + [vm] * (1 + len(consts)),
        out_specs=(vm, vm, vm),
        scratch_shapes=[
            *[pltpu.VMEM((2,) + c.shape, BF16) for c in consts[:6]],
            pltpu.VMEM((rows, rows_z), BF16),
            pltpu.VMEM((rows, 128), jnp.int32),
            big,
            big,
            big,
            big,
            pltpu.VMEM((rows, 128), F32),
            big,
            pltpu.VMEM((rows, 128), F32),
            big,
            big,
            big,
            big,
            big,
            face,
            face,
            line,
            face,
            face,
            line,
            pltpu.VMEM((24, 128), F32),
            pltpu.VMEM((24, 128), F32),
            pltpu.VMEM((nx, 24, 128), F32),
            pltpu.VMEM((ny, 24, 128), F32),
            dma((nt + 2,)),
            dma((ROUNDS, 8)),
            dma((ROUNDS, 8)),
            dma((nx,)),
            dma((nx,)),
            dma((ny,)),
            dma((ny,)),
        ],
        compiler_params=pltpu.CompilerParams(
            collective_id=0, has_side_effects=True, vmem_limit_bytes=48 << 20
        ),
    )(
        load.reshape(rows, rows_z),
        conductivity.reshape(rows, rows_z),
        flags.reshape(rows, rows_z),
        kz,
        *consts,
    )
    return tuple(o.reshape(load.shape) for o in outs)


def solution(mesh):
    cut = P("gx", "gy", None)
    return jax.shard_map(
        functools.partial(per_device, mesh.shape["gx"], mesh.shape["gy"]),
        mesh=mesh,
        in_specs=(cut, cut, cut, cut, P()),
        out_specs=(cut, cut, cut),
        check_vma=False,
    )
```

```python
import functools

import jax
import jax.numpy as jnp
import numpy as np
from jax import lax
from jax.experimental import pallas as pl
from jax.experimental.pallas import tpu as pltpu
from jax.sharding import PartitionSpec as P

NREG = 3
CENTER = 24.0
HALF = 23.0
RHO0 = HALF / CENTER
RHO1 = 1.0 / (2.0 * CENTER / HALF - RHO0)
RHO2 = 1.0 / (2.0 * CENTER / HALF - RHO1)
C1, E1 = RHO1 * RHO0, 2.0 * RHO1 / HALF
C2, E2 = RHO2 * RHO1, 2.0 * RHO2 / HALF
MESH = pl.DeviceIdType.MESH
F32, BF16 = jnp.float32, jnp.bfloat16
DIRS = ((-1, 0), (1, 0), (0, -1), (0, 1), (-1, -1), (-1, 1), (1, -1), (1, 1))
OPP = (1, 0, 3, 2, 7, 6, 5, 4)
ROUNDS = 7


def gll_tables():
    nodes = np.array(
        [
            -1.0,
            -0.8717401485096066,
            -0.5917001814331423,
            -0.2092992179024789,
            0.2092992179024789,
            0.5917001814331423,
            0.8717401485096066,
            1.0,
        ]
    )
    prev, now = np.ones(8), nodes.copy()
    for degree in range(1, 7):
        prev, now = now, ((2 * degree + 1) * nodes * now - degree * prev) / (degree + 1)
    weights = 2.0 / (56.0 * now**2)
    diff = np.zeros((8, 8))
    for a in range(8):
        for b in range(8):
            if a != b:
                diff[a, b] = now[a] / (now[b] * (nodes[a] - nodes[b]))
    diff[0, 0], diff[7, 7] = -14.0, 14.0
    return diff.astype(np.float32), weights.astype(np.float32)


def table(rows_y):
    d, w = gll_tables()
    lane = np.arange(128)
    by_y, by_x = lane % 8, lane // rows_y % 8
    parts = [m[:, by_y] for m in (d, d.T, d * d, (d * d).T)]
    parts += [m[:, by_x] for m in (d, d.T, (d * d).T)]
    quad = (w[:, None, None] * np.tile(w, rows_y // 8)[None, :, None]) * np.tile(w, 16)
    return np.concatenate(parts + [quad.reshape(8 * rows_y, 128)], 0).astype(np.float32)


def split(v):
    hi = v.astype(BF16)
    return hi, (v - hi.astype(F32)).astype(BF16)


def dot(a, b):
    return jnp.dot(a, b, preferred_element_type=F32)


def left3(m, parts):
    hi, lo = parts
    return dot(m[...], jnp.concatenate([hi, lo, hi], 0))


def right3(parts, m):
    hi, lo = parts
    return dot(jnp.concatenate([hi, lo, hi], 1), m[...])


def sum_z(tiles):
    n = len(tiles)
    lane = lax.broadcasted_iota(jnp.int32, tiles[0].shape, 1)
    ups = [pltpu.roll(w, 127, 1) for w in tiles]
    downs = [pltpu.roll(w, 1, 1) for w in tiles]
    out = []
    for t, w in enumerate(tiles):
        zero = jnp.zeros_like(w)
        up = jnp.where(lane == 127, ups[t + 1] if t + 1 < n else zero, ups[t])
        down = jnp.where(lane == 0, downs[t - 1] if t > 0 else zero, downs[t])
        out.append(w + jnp.where((lane & 7) == 7, up, jnp.where((lane & 7) == 0, down, zero)))
    return out


def sum_rows(face):
    row = lax.broadcasted_iota(jnp.int32, face.shape, 0)
    up, down = pltpu.roll(face, 15, 0), pltpu.roll(face, 1, 0)
    zero = jnp.zeros_like(face)
    return face + jnp.where(row == 7, up, jnp.where(row == 8, down, zero))


def kernel(
    nx,
    ny,
    load_h,
    cond_h,
    flag_h,
    region,
    kappa,
    tab,
    sol_o,
    res_o,
    dir_o,
    fwd,
    back,
    zfwd,
    zback,
    dxy,
    dz,
    cond,
    flag,
    wbuf,
    wbuf2,
    coef,
    reac,
    keep,
    dinv,
    dface,
    mrow,
    rvec,
    uvec,
    vec,
    r0,
    z0,
    sx,
    sy,
    sc,
    rx,
    ry,
    rc,
    part,
    part2,
    arx,
    ary,
    in_sem,
    send_sem,
    recv_sem,
    ax_send,
    ax_recv,
    ay_send,
    ay_recv,
    out_sem,
):
    mx, my = lax.axis_index("gx"), lax.axis_index("gy")
    rows = 256
    nt = wbuf.shape[0]

    copies = [
        pltpu.make_async_copy(
            load_h.at[:, pl.ds(128 * t, 128)], wbuf.at[t], in_sem.at[t]
        )
        for t in range(nt)
    ]
    copies.append(pltpu.make_async_copy(cond_h, cond, in_sem.at[nt]))
    copies.append(pltpu.make_async_copy(flag_h.at[:, pl.ds(0, 128)], flag, in_sem.at[nt + 1]))
    for c in copies:
        c.start()

    rx[...] = jnp.zeros_like(rx)
    ry[...] = jnp.zeros_like(ry)
    rc[...] = jnp.zeros_like(rc)

    def inside(dx, dy):
        ok = None
        for d, m, n in ((dx, mx, nx), (dy, my, ny)):
            if d:
                c = m > 0 if d < 0 else m < n - 1
                ok = c if ok is None else jnp.logical_and(ok, c)
        return ok

    barrier = pltpu.get_barrier_semaphore()
    for d in range(1, nx):
        pl.semaphore_signal(
            barrier, inc=1, device_id=((mx + d) % nx, my), device_id_type=MESH
        )
    for d in range(1, ny):
        pl.semaphore_signal(
            barrier, inc=1, device_id=(mx, (my + d) % ny), device_id_type=MESH
        )
    for dx, dy in DIRS[4:]:

        @pl.when(inside(dx, dy))
        def _():
            pl.semaphore_signal(
                barrier, inc=1, device_id=(mx + dx, my + dy), device_id_type=MESH
            )

    rr = lax.broadcasted_iota(jnp.int32, (rows, rows), 0)
    cc = lax.broadcasted_iota(jnp.int32, (rows, rows), 1)
    on_y = (rr >> 3) == (cc >> 3)
    on_x = ((rr & 15) == (cc & 15)) & ((rr >> 7) == (cc >> 7))

    def y_matrix(n):
        p = jnp.concatenate([tab[8 * n : 8 * n + 8, :]] * (rows // 8), 0)
        return jnp.where(on_y, jnp.concatenate([p, p], 1), 0.0)

    def x_matrix(n):
        p = [jnp.broadcast_to(tab[8 * n + a : 8 * n + a + 1, :], (16, 128)) for a in range(8)]
        p = jnp.concatenate(p + p, 0)
        return jnp.where(on_x, jnp.concatenate([p, p], 1), 0.0)

    hi, lo = split(x_matrix(6) + y_matrix(3))
    for n, m in enumerate((hi, hi, lo)):
        dxy[:, rows * n : rows * (n + 1)] = m
    hi, lo = split(y_matrix(2))
    for n, m in enumerate((hi, hi, lo)):
        dz[rows * n : rows * (n + 1), :] = m
    hi, lo = split(y_matrix(0))
    for n, m in enumerate((hi, hi, lo)):
        fwd[rows:, rows * n : rows * (n + 1)] = m
        zback[rows * n : rows * (n + 1), :] = m
    hi, lo = split(y_matrix(1))
    for n, m in enumerate((hi, hi, lo)):
        back[:, rows * (2 * n + 1) : rows * (2 * n + 2)] = m
        zfwd[rows * n : rows * (n + 1), :] = m
    hi, lo = split(x_matrix(4))
    for n, m in enumerate((hi, hi, lo)):
        fwd[:rows, rows * n : rows * (n + 1)] = m
    hi, lo = split(x_matrix(5))
    for n, m in enumerate((hi, hi, lo)):
        back[:, rows * 2 * n : rows * (2 * n + 1)] = m

    ids = jnp.concatenate(
        [
            jnp.broadcast_to(region[ex, ey : ey + 1, :], (8, region.shape[2]))
            for ex in range(2)
            for ey in range(2)
        ],
        0,
    )
    kap = jnp.zeros(ids.shape, F32)
    for n in range(NREG):
        kap = jnp.where(ids == n, kappa[n], kap)
    k_hi, k_rest = kap.astype(BF16), kap - kap.astype(BF16).astype(F32)
    k_mid, k_lo = split(k_rest)
    el = lax.broadcasted_iota(jnp.int32, (ids.shape[1], 128 * nt), 0)
    at = lax.broadcasted_iota(jnp.int32, (ids.shape[1], 128 * nt), 1) >> 3
    spread = jnp.where(el == at, 1.0, 0.0).astype(BF16)
    kz = dot(k_hi, spread) + dot(k_mid, spread) + dot(k_lo, spread)
    q0 = tab[56:, :]
    quad = jnp.concatenate([q0, q0], 0)

    peers = jnp.int32(nx - 1 + ny - 1)
    for dx, dy in DIRS[4:]:
        peers = peers + inside(dx, dy).astype(jnp.int32)
    pl.semaphore_wait(barrier, peers)

    def ends(k, i):
        if i < 2:
            return sx.at[k, i], rx.at[k, OPP[i]], rx.at[k, i]
        if i < 4:
            return sy.at[k, i - 2], ry.at[k, OPP[i] - 2], ry.at[k, i - 2]
        return sc.at[k, i - 4], rc.at[k, OPP[i] - 4], rc.at[k, i - 4]

    def start(k, w):
        for side, row in ((0, 0), (1, rows - 16)):
            tiles = sum_z([w[t, row : row + 16, :] for t in range(nt)])
            for t in range(nt):
                face = sum_rows(tiles[t])
                sx[k, side, t] = face
                sc[k, 2 * side, t : t + 1, :] = face[0:1, :]
                sc[k, 2 * side + 1, t : t + 1, :] = face[15:16, :]
        for side, row in ((0, 0), (1, 15)):
            tiles = sum_z([w[t, pl.ds(row, 16, stride=16), :] for t in range(nt)])
            for t in range(nt):
                sy[k, side, t] = sum_rows(tiles[t])
        for i, (dx, dy) in enumerate(DIRS):

            @pl.when(inside(dx, dy))
            def _():
                src, dst, _ = ends(k, i)
                pltpu.make_async_remote_copy(
                    src_ref=src,
                    dst_ref=dst,
                    send_sem=send_sem.at[k, i],
                    recv_sem=recv_sem.at[k, OPP[i]],
                    device_id=(mx + dx, my + dy),
                    device_id_type=MESH,
                ).start()

    def inner(w):
        for b in range(0, rows, 32):
            tiles = sum_z([w[t, b : b + 32, :] for t in range(nt)])
            for t in range(nt):
                w[t, b : b + 32, :] = tiles[t]
        for t in range(nt):
            s = w[t, 112:128, :] + w[t, 128:144, :]
            w[t, 112:128, :] = s
            w[t, 128:144, :] = s
            s = w[t, pl.ds(7, 16, stride=16), :] + w[t, pl.ds(8, 16, stride=16), :]
            w[t, pl.ds(7, 16, stride=16), :] = s
            w[t, pl.ds(8, 16, stride=16), :] = s

    def wait(k):
        for i, (dx, dy) in enumerate(DIRS):

            @pl.when(inside(dx, dy))
            def _():
                src, _, dst = ends(k, i)
                c = pltpu.make_async_remote_copy(
                    src_ref=src,
                    dst_ref=dst,
                    send_sem=send_sem.at[k, i],
                    recv_sem=recv_sem.at[k, i],
                    device_id=(mx + dx, my + dy),
                    device_id_type=MESH,
                )
                c.wait_recv()
                c.wait_send()

    def faces(t):
        return (
            (slice(0, 16), 0),
            (slice(rows - 16, rows), 1),
            (pl.ds(0, 16, stride=16), 2),
            (pl.ds(15, 16, stride=16), 3),
        )

    row16 = lax.broadcasted_iota(jnp.int32, (16, 128), 0)

    def arrived(k, f, t):
        if f >= 2:
            return ry[k, f - 2, t]
        low, high = rc[k, 2 * f, t : t + 1, :], rc[k, 2 * f + 1, t : t + 1, :]
        zero = jnp.zeros((16, 128), F32)
        return rx[k, f, t] + jnp.where(row16 == 0, low, jnp.where(row16 == 15, high, zero))

    def finish(k, w):
        wait(k)
        for t in range(nt):
            for where, f in faces(t):
                w[t, where, :] += arrived(k, f, t)

    def correct(k, scale, also=None):
        wait(k)
        for t in range(nt):
            for where, f in faces(t):
                h = arrived(k, f, t)
                vec[t, where, :] += (scale * dface[f, t]) * h
                if also is not None:
                    also[t, where, :] += keep[where, :] * h if t == 0 else h

    for c in copies[:nt]:
        c.wait()
    start(0, wbuf)
    copies[nt].wait()
    copies[nt + 1].wait()
    for t in range(nt):
        coef[t] = quad * cond[:, 128 * t : 128 * (t + 1)].astype(F32)
        kt = kz[:, 128 * t : 128 * (t + 1)]
        kap = jnp.concatenate([kt[0:16]] * 8 + [kt[16:32]] * 8, 0)
        reac[t] = quad * kap
    lane = lax.broadcasted_iota(jnp.int32, (rows, 128), 1)
    keep[...] = jnp.where(lane == 0, (1 - flag[...]).astype(F32), 1.0)

    for c in range(nt // 2):
        cc = jnp.concatenate([coef[2 * c], coef[2 * c + 1]], 1)
        parts = split(cc)
        out = left3(dxy, parts) + right3(parts, dz)
        for h in range(2):
            t = 2 * c + h
            wbuf2[t] = out[:, 128 * h : 128 * (h + 1)] + reac[t]
    start(1, wbuf2)

    row = lax.broadcasted_iota(jnp.int32, (rows, 128), 0)
    px, py = mx * 16 + (row >> 4), my * 16 + (row & 15)
    share = jnp.ones((rows, 128), F32)
    for p, total in ((px, 16 * nx), (py, 16 * ny)):
        shared = ((p & 7) == 7) & (p != total - 1) | ((p & 7) == 0) & (p != 0)
        share = share * jnp.where(shared, 0.5, 1.0)
    mrow[...] = share
    part[...] = jnp.zeros_like(part)

    def lane_share(t):
        z = lax.broadcasted_iota(jnp.int32, (8, 128), 1) + 128 * t
        shared = ((z & 7) == 7) & (z != 128 * nt - 1) | ((z & 7) == 0) & (z != 0)
        return jnp.where(shared, 0.5, 1.0)

    def add_part(slot, t, prod):
        s = jnp.sum((prod * mrow[...]).reshape(rows // 8, 8, 128), axis=0)
        part[8 * slot : 8 * slot + 8, :] += s * lane_share(t)

    inner(wbuf)
    inner(wbuf2)
    finish(0, wbuf)
    finish(1, wbuf2)
    for t in range(nt):
        res, dia = wbuf[t], wbuf2[t]
        if t == 0:
            res = keep[...] * res
            dia = keep[...] * dia + (1.0 - keep[...])
        inv = 1.0 / dia
        r0[t] = res
        dinv[t] = inv
        vec[t] = res * inv * (1.0 / CENTER)
        for where, f in faces(t):
            inv = dinv[t, where, :]
            dface[f, t] = keep[where, :] * inv if t == 0 else inv

    def apply(k):
        for c in range(nt // 2):
            first = vec[2 * c]
            if c == 0:
                first = keep[...] * first
            v = jnp.concatenate([first, vec[2 * c + 1]], 1)
            cc = jnp.concatenate([coef[2 * c], coef[2 * c + 1]], 1)
            rr = jnp.concatenate([reac[2 * c], reac[2 * c + 1]], 1)
            parts = split(v)
            gxy = left3(fwd, parts)
            gz = right3(parts, zfwd)
            fxy = split(gxy * jnp.concatenate([cc, cc], 0))
            fz = split(gz * cc)
            out = left3(back, fxy) + right3(fz, zback) + rr * v
            wbuf[2 * c] = out[:, :128]
            wbuf[2 * c + 1] = out[:, 128:]
        start(k, wbuf)
        inner(wbuf)

    def image_of(t):
        out = wbuf[t]
        if t == 0:
            out = keep[...] * out + (1.0 - keep[...]) * vec[t]
        return out

    def reduce_copy(src, dst, sems, slot, dev):
        return pltpu.make_async_remote_copy(
            src_ref=src,
            dst_ref=dst,
            send_sem=sems[0].at[slot[0]],
            recv_sem=sems[1].at[slot[1]],
            device_id=dev,
            device_id_type=MESH,
        )

    k1 = 1.0 + C1 + CENTER * E1
    k2, k3 = 1.0 + C2, CENTER * E2 - C2
    apply(2)
    for t in range(nt):
        a0 = vec[t]
        new = k1 * a0 - (E1 * dinv[t]) * image_of(t)
        uvec[t] = a0
        vec[t] = new
    correct(2, -E1)
    apply(3)
    for t in range(nt):
        vec[t] = k2 * vec[t] + k3 * uvec[t] - (E2 * dinv[t]) * image_of(t)
    correct(3, -E2)
    apply(4)
    for t in range(nt):
        z, im = vec[t], image_of(t)
        z0[t] = z
        rvec[t] = im
        vec[t] = im * dinv[t] * (1.0 / CENTER)
        add_part(0, t, r0[t] * z)
    correct(4, 1.0 / CENTER, rvec)
    apply(5)
    for t in range(nt):
        add_part(1, t, rvec[t] * z0[t])
    finish(5, wbuf)
    for t in range(nt):
        a0, im, az = vec[t], rvec[t], image_of(t)
        a1 = k1 * a0 - (E1 * dinv[t]) * az
        uvec[t] = a0
        vec[t] = a1
        add_part(2, t, im * (k2 * a1 + k3 * a0) - (CENTER * E2) * (az * a1))
    arx[mx] = part[...]
    for d in range(1, nx):
        to = (mx + d) % nx
        reduce_copy(part, arx.at[mx], (ax_send, ax_recv), (d, mx), (to, my)).start()
    apply(6)
    for d in range(1, nx):
        frm = (mx + nx - d) % nx
        c = reduce_copy(part, arx.at[frm], (ax_send, ax_recv), (d, frm), (frm, my))
        c.wait_recv()
        c.wait_send()
    total = arx[0]
    for d in range(1, nx):
        total = total + arx[d]
    part2[...] = total
    ary[my] = total
    for d in range(1, ny):
        to = (my + d) % ny
        reduce_copy(part2, ary.at[my], (ay_send, ay_recv), (d, my), (mx, to)).start()
    for t in range(nt):
        vec[t] = k2 * vec[t] + k3 * uvec[t] - (E2 * dinv[t]) * image_of(t)
    correct(6, -E2)
    for d in range(1, ny):
        frm = (my + ny - d) % ny
        c = reduce_copy(part2, ary.at[frm], (ay_send, ay_recv), (d, frm), (mx, frm))
        c.wait_recv()
        c.wait_send()
    total = ary[0]
    for d in range(1, ny):
        total = total + ary[d]

    def whole(slot):
        return jnp.sum(total[8 * slot : 8 * slot + 8], axis=(0, 1), keepdims=True)

    first, curv, quadratic = whole(0), whole(1), whole(2)
    step = first / curv
    second = step * step * quadratic - first
    beta1 = 1.0 + second / first
    stores = []
    for t in range(nt):
        wbuf[t] = step * z0[t]
        wbuf2[t] = r0[t] - step * rvec[t]
        vec[t] = beta1 * z0[t] - step * vec[t]
        for n, (src, dst) in enumerate(((wbuf, sol_o), (wbuf2, res_o), (vec, dir_o))):
            c = pltpu.make_async_copy(
                src.at[t], dst.at[:, pl.ds(128 * t, 128)], out_sem.at[n, t]
            )
            c.start()
            stores.append(c)
    for c in stores:
        c.wait()


def store_kernel(a, b, c, oa, ob, oc, sem):
    copies = [
        pltpu.make_async_copy(src, dst, sem.at[n])
        for n, (src, dst) in enumerate(((a, oa), (b, ob), (c, oc)))
    ]
    for copy in copies:
        copy.start()
    for copy in copies:
        copy.wait()


def per_device(nx, ny, load, conductivity, flags, region, kappa_table):
    rows_x, rows_y, rows_z = load.shape
    rows, nt = rows_x * rows_y, rows_z // 128
    big = pltpu.VMEM((nt, rows, 128), F32)
    face = pltpu.VMEM((ROUNDS, 2, nt, 16, 128), F32)
    line = pltpu.VMEM((ROUNDS, 4, 8, 128), F32)
    vm = pl.BlockSpec(memory_space=pltpu.VMEM)
    hbm = pl.BlockSpec(memory_space=pltpu.HBM)
    out = jax.ShapeDtypeStruct((rows, rows_z), F32)
    dma = pltpu.SemaphoreType.DMA
    outs = pl.pallas_call(
        functools.partial(kernel, nx, ny),
        out_shape=(out, out, out),
        in_specs=[hbm] * 3 + [vm, pl.BlockSpec(memory_space=pltpu.SMEM), vm],
        out_specs=(hbm, hbm, hbm),
        scratch_shapes=[
            pltpu.VMEM((2 * rows, 3 * rows), BF16),
            pltpu.VMEM((rows, 6 * rows), BF16),
            pltpu.VMEM((3 * rows, rows), BF16),
            pltpu.VMEM((3 * rows, rows), BF16),
            pltpu.VMEM((rows, 3 * rows), BF16),
            pltpu.VMEM((3 * rows, rows), BF16),
            pltpu.VMEM((rows, rows_z), BF16),
            pltpu.VMEM((rows, 128), jnp.int32),
            big,
            big,
            big,
            big,
            pltpu.VMEM((rows, 128), F32),
            big,
            pltpu.VMEM((4, nt, 16, 128), F32),
            pltpu.VMEM((rows, 128), F32),
            big,
            big,
            big,
            big,
            big,
            face,
            face,
            line,
            face,
            face,
            line,
            pltpu.VMEM((24, 128), F32),
            pltpu.VMEM((24, 128), F32),
            pltpu.VMEM((nx, 24, 128), F32),
            pltpu.VMEM((ny, 24, 128), F32),
            dma((nt + 2,)),
            dma((ROUNDS, 8)),
            dma((ROUNDS, 8)),
            dma((nx,)),
            dma((nx,)),
            dma((ny,)),
            dma((ny,)),
            dma((3, nt)),
        ],
        compiler_params=pltpu.CompilerParams(
            collective_id=0, has_side_effects=True, vmem_limit_bytes=62 << 20
        ),
    )(
        load.reshape(rows, rows_z),
        conductivity.reshape(rows, rows_z),
        flags.reshape(rows, rows_z),
        region,
        kappa_table,
        jnp.asarray(table(rows_y)),
    )
    outs = pl.pallas_call(
        store_kernel,
        out_shape=(out, out, out),
        in_specs=[hbm] * 3,
        out_specs=(hbm, hbm, hbm),
        scratch_shapes=[dma((3,))],
        compiler_params=pltpu.CompilerParams(vmem_limit_bytes=62 << 20),
    )(*outs)
    return tuple(o.reshape(load.shape) for o in outs)


def solution(mesh):
    cut = P("gx", "gy", None)
    return jax.shard_map(
        functools.partial(per_device, mesh.shape["gx"], mesh.shape["gy"]),
        mesh=mesh,
        in_specs=(cut, cut, cut, cut, P()),
        out_specs=(cut, cut, cut),
        check_vma=False,
    )
```

```python
import functools

import jax
import jax.numpy as jnp
import numpy as np
from jax import lax
from jax.experimental import pallas as pl
from jax.experimental.pallas import tpu as pltpu
from jax.sharding import PartitionSpec as P

NREG = 3
CENTER = 24.0
HALF = 23.0
RHO0 = HALF / CENTER
RHO1 = 1.0 / (2.0 * CENTER / HALF - RHO0)
RHO2 = 1.0 / (2.0 * CENTER / HALF - RHO1)
C1, E1 = RHO1 * RHO0, 2.0 * RHO1 / HALF
C2, E2 = RHO2 * RHO1, 2.0 * RHO2 / HALF
MESH = pl.DeviceIdType.MESH
F32, BF16 = jnp.float32, jnp.bfloat16
DIRS = ((-1, 0), (1, 0), (0, -1), (0, 1), (-1, -1), (-1, 1), (1, -1), (1, 1))
OPP = (1, 0, 3, 2, 7, 6, 5, 4)
ROUNDS = 7


def gll_tables():
    nodes = np.array(
        [
            -1.0,
            -0.8717401485096066,
            -0.5917001814331423,
            -0.2092992179024789,
            0.2092992179024789,
            0.5917001814331423,
            0.8717401485096066,
            1.0,
        ]
    )
    prev, now = np.ones(8), nodes.copy()
    for degree in range(1, 7):
        prev, now = now, ((2 * degree + 1) * nodes * now - degree * prev) / (degree + 1)
    weights = 2.0 / (56.0 * now**2)
    diff = np.zeros((8, 8))
    for a in range(8):
        for b in range(8):
            if a != b:
                diff[a, b] = now[a] / (now[b] * (nodes[a] - nodes[b]))
    diff[0, 0], diff[7, 7] = -14.0, 14.0
    return diff.astype(np.float32), weights.astype(np.float32)


def table(rows_y):
    d, w = gll_tables()
    lane = np.arange(128)
    by_y, by_x = lane % 8, lane // rows_y % 8
    parts = [m[:, by_y] for m in (d, d.T, d * d, (d * d).T)]
    parts += [m[:, by_x] for m in (d, d.T, (d * d).T)]
    quad = (w[:, None, None] * np.tile(w, rows_y // 8)[None, :, None]) * np.tile(w, 16)
    return np.concatenate(parts + [quad.reshape(8 * rows_y, 128)], 0).astype(np.float32)


def split(v):
    hi = v.astype(BF16)
    return hi, (v - hi.astype(F32)).astype(BF16)


def dot(a, b):
    return jnp.dot(a, b, preferred_element_type=F32)


def left3(m, parts):
    hi, lo = parts
    return dot(m[...], jnp.concatenate([hi, lo, hi], 0))


def right3(parts, m):
    hi, lo = parts
    return dot(jnp.concatenate([hi, lo, hi], 1), m[...])


def sum_z(tiles):
    n = len(tiles)
    lane = lax.broadcasted_iota(jnp.int32, tiles[0].shape, 1)
    ups = [pltpu.roll(w, 127, 1) for w in tiles]
    downs = [pltpu.roll(w, 1, 1) for w in tiles]
    out = []
    for t, w in enumerate(tiles):
        zero = jnp.zeros_like(w)
        up = jnp.where(lane == 127, ups[t + 1] if t + 1 < n else zero, ups[t])
        down = jnp.where(lane == 0, downs[t - 1] if t > 0 else zero, downs[t])
        out.append(w + jnp.where((lane & 7) == 7, up, jnp.where((lane & 7) == 0, down, zero)))
    return out


def sum_rows(face):
    row = lax.broadcasted_iota(jnp.int32, face.shape, 0)
    up, down = pltpu.roll(face, 15, 0), pltpu.roll(face, 1, 0)
    zero = jnp.zeros_like(face)
    return face + jnp.where(row == 7, up, jnp.where(row == 8, down, zero))


def kernel(
    nx,
    ny,
    load_h,
    cond_h,
    flag_h,
    region,
    kappa,
    tab,
    sol_o,
    res_o,
    dir_o,
    fwd,
    back,
    zfwd,
    zback,
    dxy,
    dz,
    cond,
    flag,
    wbuf,
    wbuf2,
    coef,
    reac,
    keep,
    dinv,
    dface,
    mrow,
    rvec,
    uvec,
    vec,
    r0,
    z0,
    sx,
    sy,
    sc,
    rx,
    ry,
    rc,
    part,
    part2,
    arx,
    ary,
    in_sem,
    send_sem,
    recv_sem,
    ax_send,
    ax_recv,
    ay_send,
    ay_recv,
    out_sem,
):
    mx, my = lax.axis_index("gx"), lax.axis_index("gy")
    rows = 256
    nt = wbuf.shape[0]

    copies = [
        pltpu.make_async_copy(
            load_h.at[:, pl.ds(128 * t, 128)], wbuf.at[t], in_sem.at[t]
        )
        for t in range(nt)
    ]
    copies.append(pltpu.make_async_copy(cond_h, cond, in_sem.at[nt]))
    copies.append(pltpu.make_async_copy(flag_h.at[:, pl.ds(0, 128)], flag, in_sem.at[nt + 1]))
    for c in copies:
        c.start()

    rx[...] = jnp.zeros_like(rx)
    ry[...] = jnp.zeros_like(ry)
    rc[...] = jnp.zeros_like(rc)

    def inside(dx, dy):
        ok = None
        for d, m, n in ((dx, mx, nx), (dy, my, ny)):
            if d:
                c = m > 0 if d < 0 else m < n - 1
                ok = c if ok is None else jnp.logical_and(ok, c)
        return ok

    barrier = pltpu.get_barrier_semaphore()
    for d in range(1, nx):
        pl.semaphore_signal(
            barrier, inc=1, device_id=((mx + d) % nx, my), device_id_type=MESH
        )
    for d in range(1, ny):
        pl.semaphore_signal(
            barrier, inc=1, device_id=(mx, (my + d) % ny), device_id_type=MESH
        )
    for dx, dy in DIRS[4:]:

        @pl.when(inside(dx, dy))
        def _():
            pl.semaphore_signal(
                barrier, inc=1, device_id=(mx + dx, my + dy), device_id_type=MESH
            )

    rr = lax.broadcasted_iota(jnp.int32, (rows, rows), 0)
    cc = lax.broadcasted_iota(jnp.int32, (rows, rows), 1)
    on_y = (rr >> 3) == (cc >> 3)
    on_x = ((rr & 15) == (cc & 15)) & ((rr >> 7) == (cc >> 7))

    def y_matrix(n):
        p = jnp.concatenate([tab[8 * n : 8 * n + 8, :]] * (rows // 8), 0)
        return jnp.where(on_y, jnp.concatenate([p, p], 1), 0.0)

    def x_matrix(n):
        p = [jnp.broadcast_to(tab[8 * n + a : 8 * n + a + 1, :], (16, 128)) for a in range(8)]
        p = jnp.concatenate(p + p, 0)
        return jnp.where(on_x, jnp.concatenate([p, p], 1), 0.0)

    hi, lo = split(x_matrix(6) + y_matrix(3))
    for n, m in enumerate((hi, hi, lo)):
        dxy[:, rows * n : rows * (n + 1)] = m
    hi, lo = split(y_matrix(2))
    for n, m in enumerate((hi, hi, lo)):
        dz[rows * n : rows * (n + 1), :] = m
    hi, lo = split(y_matrix(0))
    for n, m in enumerate((hi, hi, lo)):
        fwd[rows:, rows * n : rows * (n + 1)] = m
        zback[rows * n : rows * (n + 1), :] = m
    hi, lo = split(y_matrix(1))
    for n, m in enumerate((hi, hi, lo)):
        back[:, rows * (2 * n + 1) : rows * (2 * n + 2)] = m
        zfwd[rows * n : rows * (n + 1), :] = m
    hi, lo = split(x_matrix(4))
    for n, m in enumerate((hi, hi, lo)):
        fwd[:rows, rows * n : rows * (n + 1)] = m
    hi, lo = split(x_matrix(5))
    for n, m in enumerate((hi, hi, lo)):
        back[:, rows * 2 * n : rows * (2 * n + 1)] = m

    ids = jnp.concatenate(
        [
            jnp.broadcast_to(region[ex, ey : ey + 1, :], (8, region.shape[2]))
            for ex in range(2)
            for ey in range(2)
        ],
        0,
    )
    kap = jnp.zeros(ids.shape, F32)
    for n in range(NREG):
        kap = jnp.where(ids == n, kappa[n], kap)
    k_hi, k_rest = kap.astype(BF16), kap - kap.astype(BF16).astype(F32)
    k_mid, k_lo = split(k_rest)
    el = lax.broadcasted_iota(jnp.int32, (ids.shape[1], 128 * nt), 0)
    at = lax.broadcasted_iota(jnp.int32, (ids.shape[1], 128 * nt), 1) >> 3
    spread = jnp.where(el == at, 1.0, 0.0).astype(BF16)
    kz = dot(k_hi, spread) + dot(k_mid, spread) + dot(k_lo, spread)
    q0 = tab[56:, :]
    quad = jnp.concatenate([q0, q0], 0)

    peers = jnp.int32(nx - 1 + ny - 1)
    for dx, dy in DIRS[4:]:
        peers = peers + inside(dx, dy).astype(jnp.int32)
    pl.semaphore_wait(barrier, peers)

    def ends(k, i):
        if i < 2:
            return sx.at[k, i], rx.at[k, OPP[i]], rx.at[k, i]
        if i < 4:
            return sy.at[k, i - 2], ry.at[k, OPP[i] - 2], ry.at[k, i - 2]
        return sc.at[k, i - 4], rc.at[k, OPP[i] - 4], rc.at[k, i - 4]

    def start(k, w):
        for side, row in ((0, 0), (1, rows - 16)):
            tiles = sum_z([w[t, row : row + 16, :] for t in range(nt)])
            for t in range(nt):
                face = sum_rows(tiles[t])
                sx[k, side, t] = face
                sc[k, 2 * side, t : t + 1, :] = face[0:1, :]
                sc[k, 2 * side + 1, t : t + 1, :] = face[15:16, :]
        for side, row in ((0, 0), (1, 15)):
            tiles = sum_z([w[t, pl.ds(row, 16, stride=16), :] for t in range(nt)])
            for t in range(nt):
                sy[k, side, t] = sum_rows(tiles[t])
        for i, (dx, dy) in enumerate(DIRS):

            @pl.when(inside(dx, dy))
            def _():
                src, dst, _ = ends(k, i)
                pltpu.make_async_remote_copy(
                    src_ref=src,
                    dst_ref=dst,
                    send_sem=send_sem.at[k, i],
                    recv_sem=recv_sem.at[k, OPP[i]],
                    device_id=(mx + dx, my + dy),
                    device_id_type=MESH,
                ).start()

    def inner(w):
        for b in range(0, rows, 32):
            tiles = sum_z([w[t, b : b + 32, :] for t in range(nt)])
            for t in range(nt):
                w[t, b : b + 32, :] = tiles[t]
        for t in range(nt):
            s = w[t, 112:128, :] + w[t, 128:144, :]
            w[t, 112:128, :] = s
            w[t, 128:144, :] = s
            s = w[t, pl.ds(7, 16, stride=16), :] + w[t, pl.ds(8, 16, stride=16), :]
            w[t, pl.ds(7, 16, stride=16), :] = s
            w[t, pl.ds(8, 16, stride=16), :] = s

    def wait(k):
        for i, (dx, dy) in enumerate(DIRS):

            @pl.when(inside(dx, dy))
            def _():
                src, _, dst = ends(k, i)
                c = pltpu.make_async_remote_copy(
                    src_ref=src,
                    dst_ref=dst,
                    send_sem=send_sem.at[k, i],
                    recv_sem=recv_sem.at[k, i],
                    device_id=(mx + dx, my + dy),
                    device_id_type=MESH,
                )
                c.wait_recv()
                c.wait_send()

    def faces(t):
        return (
            (slice(0, 16), 0),
            (slice(rows - 16, rows), 1),
            (pl.ds(0, 16, stride=16), 2),
            (pl.ds(15, 16, stride=16), 3),
        )

    row16 = lax.broadcasted_iota(jnp.int32, (16, 128), 0)

    def arrived(k, f, t):
        if f >= 2:
            return ry[k, f - 2, t]
        low, high = rc[k, 2 * f, t : t + 1, :], rc[k, 2 * f + 1, t : t + 1, :]
        zero = jnp.zeros((16, 128), F32)
        return rx[k, f, t] + jnp.where(row16 == 0, low, jnp.where(row16 == 15, high, zero))

    def finish(k, w):
        wait(k)
        for t in range(nt):
            for where, f in faces(t):
                w[t, where, :] += arrived(k, f, t)

    def correct(k, scale, also=None):
        wait(k)
        for t in range(nt):
            for where, f in faces(t):
                h = arrived(k, f, t)
                vec[t, where, :] += (scale * dface[f, t]) * h
                if also is not None:
                    also[t, where, :] += keep[where, :] * h if t == 0 else h

    for c in copies[:nt]:
        c.wait()
    start(0, wbuf)
    copies[nt].wait()
    copies[nt + 1].wait()
    for t in range(nt):
        coef[t] = quad * cond[:, 128 * t : 128 * (t + 1)].astype(F32)
        kt = kz[:, 128 * t : 128 * (t + 1)]
        kap = jnp.concatenate([kt[0:16]] * 8 + [kt[16:32]] * 8, 0)
        reac[t] = quad * kap
    lane = lax.broadcasted_iota(jnp.int32, (rows, 128), 1)
    keep[...] = jnp.where(lane == 0, (1 - flag[...]).astype(F32), 1.0)

    for c in range(nt // 2):
        cc = jnp.concatenate([coef[2 * c], coef[2 * c + 1]], 1)
        parts = split(cc)
        out = left3(dxy, parts) + right3(parts, dz)
        for h in range(2):
            t = 2 * c + h
            wbuf2[t] = out[:, 128 * h : 128 * (h + 1)] + reac[t]
    start(1, wbuf2)

    row = lax.broadcasted_iota(jnp.int32, (rows, 128), 0)
    px, py = mx * 16 + (row >> 4), my * 16 + (row & 15)
    share = jnp.ones((rows, 128), F32)
    for p, total in ((px, 16 * nx), (py, 16 * ny)):
        shared = ((p & 7) == 7) & (p != total - 1) | ((p & 7) == 0) & (p != 0)
        share = share * jnp.where(shared, 0.5, 1.0)
    mrow[...] = share
    part[...] = jnp.zeros_like(part)

    def lane_share(t):
        z = lax.broadcasted_iota(jnp.int32, (8, 128), 1) + 128 * t
        shared = ((z & 7) == 7) & (z != 128 * nt - 1) | ((z & 7) == 0) & (z != 0)
        return jnp.where(shared, 0.5, 1.0)

    def add_part(slot, t, prod):
        s = jnp.sum((prod * mrow[...]).reshape(rows // 8, 8, 128), axis=0)
        part[8 * slot : 8 * slot + 8, :] += s * lane_share(t)

    inner(wbuf)
    inner(wbuf2)
    finish(0, wbuf)
    finish(1, wbuf2)
    for t in range(nt):
        res, dia = wbuf[t], wbuf2[t]
        if t == 0:
            res = keep[...] * res
            dia = keep[...] * dia + (1.0 - keep[...])
        inv = 1.0 / dia
        r0[t] = res
        dinv[t] = inv
        vec[t] = res * inv * (1.0 / CENTER)
        for where, f in faces(t):
            inv = dinv[t, where, :]
            dface[f, t] = keep[where, :] * inv if t == 0 else inv

    def apply(k):
        for c in range(nt // 2):
            first = vec[2 * c]
            if c == 0:
                first = keep[...] * first
            v = jnp.concatenate([first, vec[2 * c + 1]], 1)
            cc = jnp.concatenate([coef[2 * c], coef[2 * c + 1]], 1)
            rr = jnp.concatenate([reac[2 * c], reac[2 * c + 1]], 1)
            parts = split(v)
            gxy = left3(fwd, parts)
            gz = right3(parts, zfwd)
            fxy = split(gxy * jnp.concatenate([cc, cc], 0))
            fz = split(gz * cc)
            out = left3(back, fxy) + right3(fz, zback) + rr * v
            wbuf[2 * c] = out[:, :128]
            wbuf[2 * c + 1] = out[:, 128:]
        start(k, wbuf)
        inner(wbuf)

    def image_of(t):
        out = wbuf[t]
        if t == 0:
            out = keep[...] * out + (1.0 - keep[...]) * vec[t]
        return out

    def reduce_copy(src, dst, sems, slot, dev):
        return pltpu.make_async_remote_copy(
            src_ref=src,
            dst_ref=dst,
            send_sem=sems[0].at[slot[0]],
            recv_sem=sems[1].at[slot[1]],
            device_id=dev,
            device_id_type=MESH,
        )

    k1 = 1.0 + C1 + CENTER * E1
    k2, k3 = 1.0 + C2, CENTER * E2 - C2
    apply(2)
    for t in range(nt):
        a0 = vec[t]
        new = k1 * a0 - (E1 * dinv[t]) * image_of(t)
        uvec[t] = a0
        vec[t] = new
    correct(2, -E1)
    apply(3)
    for t in range(nt):
        vec[t] = k2 * vec[t] + k3 * uvec[t] - (E2 * dinv[t]) * image_of(t)
    correct(3, -E2)
    apply(4)
    for t in range(nt):
        z, im = vec[t], image_of(t)
        z0[t] = z
        rvec[t] = im
        vec[t] = im * dinv[t] * (1.0 / CENTER)
        add_part(0, t, r0[t] * z)
    correct(4, 1.0 / CENTER, rvec)
    apply(5)
    for t in range(nt):
        add_part(1, t, rvec[t] * z0[t])
    finish(5, wbuf)
    for t in range(nt):
        a0, im, az = vec[t], rvec[t], image_of(t)
        a1 = k1 * a0 - (E1 * dinv[t]) * az
        uvec[t] = a0
        vec[t] = a1
        add_part(2, t, im * (k2 * a1 + k3 * a0) - (CENTER * E2) * (az * a1))
    arx[mx] = part[...]
    for d in range(1, nx):
        to = (mx + d) % nx
        reduce_copy(part, arx.at[mx], (ax_send, ax_recv), (d, mx), (to, my)).start()
    apply(6)
    for d in range(1, nx):
        frm = (mx + nx - d) % nx
        c = reduce_copy(part, arx.at[frm], (ax_send, ax_recv), (d, frm), (frm, my))
        c.wait_recv()
        c.wait_send()
    total = arx[0]
    for d in range(1, nx):
        total = total + arx[d]
    part2[...] = total
    ary[my] = total
    for d in range(1, ny):
        to = (my + d) % ny
        reduce_copy(part2, ary.at[my], (ay_send, ay_recv), (d, my), (mx, to)).start()
    for t in range(nt):
        vec[t] = k2 * vec[t] + k3 * uvec[t] - (E2 * dinv[t]) * image_of(t)
    correct(6, -E2)
    for d in range(1, ny):
        frm = (my + ny - d) % ny
        c = reduce_copy(part2, ary.at[frm], (ay_send, ay_recv), (d, frm), (mx, frm))
        c.wait_recv()
        c.wait_send()
    total = ary[0]
    for d in range(1, ny):
        total = total + ary[d]

    def whole(slot):
        return jnp.sum(total[8 * slot : 8 * slot + 8], axis=(0, 1), keepdims=True)

    first, curv, quadratic = whole(0), whole(1), whole(2)
    step = first / curv
    second = step * step * quadratic - first
    beta1 = 1.0 + second / first
    stores = []
    for t in range(nt):
        wbuf[t] = step * z0[t]
        wbuf2[t] = r0[t] - step * rvec[t]
        vec[t] = beta1 * z0[t] - step * vec[t]
        for n, (src, dst) in enumerate(((wbuf, sol_o), (wbuf2, res_o), (vec, dir_o))):
            c = pltpu.make_async_copy(
                src.at[t], dst.at[:, pl.ds(128 * t, 128)], out_sem.at[n, t]
            )
            c.start()
            stores.append(c)
    for c in stores:
        c.wait()


def store_kernel(a, b, c, oa, ob, oc, buf, in_sem, out_sem):
    rows = a.shape[0] // 2
    ins, outs = [], []
    for n, (src, dst) in enumerate(((a, oa), (b, ob), (c, oc))):
        for h in range(2):
            part = pl.ds(rows * h, rows)
            ins.append(
                pltpu.make_async_copy(src.at[part, :], buf.at[n, h], in_sem.at[n, h])
            )
            outs.append(
                pltpu.make_async_copy(buf.at[n, h], dst.at[part, :], out_sem.at[n, h])
            )
    for copy in ins:
        copy.start()
    for copy, out in zip(ins, outs):
        copy.wait()
        out.start()
    for out in outs:
        out.wait()


def per_device(nx, ny, load, conductivity, flags, region, kappa_table):
    rows_x, rows_y, rows_z = load.shape
    rows, nt = rows_x * rows_y, rows_z // 128
    big = pltpu.VMEM((nt, rows, 128), F32)
    face = pltpu.VMEM((ROUNDS, 2, nt, 16, 128), F32)
    line = pltpu.VMEM((ROUNDS, 4, 8, 128), F32)
    vm = pl.BlockSpec(memory_space=pltpu.VMEM)
    hbm = pl.BlockSpec(memory_space=pltpu.HBM)
    out = jax.ShapeDtypeStruct((rows, rows_z), F32)
    dma = pltpu.SemaphoreType.DMA
    outs = pl.pallas_call(
        functools.partial(kernel, nx, ny),
        out_shape=(out, out, out),
        in_specs=[hbm] * 3 + [vm, pl.BlockSpec(memory_space=pltpu.SMEM), vm],
        out_specs=(hbm, hbm, hbm),
        scratch_shapes=[
            pltpu.VMEM((2 * rows, 3 * rows), BF16),
            pltpu.VMEM((rows, 6 * rows), BF16),
            pltpu.VMEM((3 * rows, rows), BF16),
            pltpu.VMEM((3 * rows, rows), BF16),
            pltpu.VMEM((rows, 3 * rows), BF16),
            pltpu.VMEM((3 * rows, rows), BF16),
            pltpu.VMEM((rows, rows_z), BF16),
            pltpu.VMEM((rows, 128), jnp.int32),
            big,
            big,
            big,
            big,
            pltpu.VMEM((rows, 128), F32),
            big,
            pltpu.VMEM((4, nt, 16, 128), F32),
            pltpu.VMEM((rows, 128), F32),
            big,
            big,
            big,
            big,
            big,
            face,
            face,
            line,
            face,
            face,
            line,
            pltpu.VMEM((24, 128), F32),
            pltpu.VMEM((24, 128), F32),
            pltpu.VMEM((nx, 24, 128), F32),
            pltpu.VMEM((ny, 24, 128), F32),
            dma((nt + 2,)),
            dma((ROUNDS, 8)),
            dma((ROUNDS, 8)),
            dma((nx,)),
            dma((nx,)),
            dma((ny,)),
            dma((ny,)),
            dma((3, nt)),
        ],
        compiler_params=pltpu.CompilerParams(
            collective_id=0, has_side_effects=True, vmem_limit_bytes=62 << 20
        ),
    )(
        load.reshape(rows, rows_z),
        conductivity.reshape(rows, rows_z),
        flags.reshape(rows, rows_z),
        region,
        kappa_table,
        jnp.asarray(table(rows_y)),
    )
    outs = pl.pallas_call(
        store_kernel,
        out_shape=(out, out, out),
        in_specs=[hbm] * 3,
        out_specs=(hbm, hbm, hbm),
        scratch_shapes=[
            pltpu.VMEM((3, 2, rows // 2, rows_z), F32),
            dma((3, 2)),
            dma((3, 2)),
        ],
        compiler_params=pltpu.CompilerParams(vmem_limit_bytes=62 << 20),
    )(*outs)
    return tuple(o.reshape(load.shape) for o in outs)


def solution(mesh):
    cut = P("gx", "gy", None)
    return jax.shard_map(
        functools.partial(per_device, mesh.shape["gx"], mesh.shape["gy"]),
        mesh=mesh,
        in_specs=(cut, cut, cut, cut, P()),
        out_specs=(cut, cut, cut),
        check_vma=False,
    )
```

```python
import functools

import jax
import jax.numpy as jnp
import numpy as np
from jax import lax
from jax.experimental import pallas as pl
from jax.experimental.pallas import tpu as pltpu
from jax.sharding import PartitionSpec as P

NREG = 3
CENTER = 24.0
HALF = 23.0
RHO0 = HALF / CENTER
RHO1 = 1.0 / (2.0 * CENTER / HALF - RHO0)
RHO2 = 1.0 / (2.0 * CENTER / HALF - RHO1)
C1, E1 = RHO1 * RHO0, 2.0 * RHO1 / HALF
C2, E2 = RHO2 * RHO1, 2.0 * RHO2 / HALF
MESH = pl.DeviceIdType.MESH
F32, BF16 = jnp.float32, jnp.bfloat16
DIRS = ((-1, 0), (1, 0), (0, -1), (0, 1), (-1, -1), (-1, 1), (1, -1), (1, 1))
OPP = (1, 0, 3, 2, 7, 6, 5, 4)
ROUNDS = 7


def gll_tables():
    nodes = np.array(
        [
            -1.0,
            -0.8717401485096066,
            -0.5917001814331423,
            -0.2092992179024789,
            0.2092992179024789,
            0.5917001814331423,
            0.8717401485096066,
            1.0,
        ]
    )
    prev, now = np.ones(8), nodes.copy()
    for degree in range(1, 7):
        prev, now = now, ((2 * degree + 1) * nodes * now - degree * prev) / (degree + 1)
    weights = 2.0 / (56.0 * now**2)
    diff = np.zeros((8, 8))
    for a in range(8):
        for b in range(8):
            if a != b:
                diff[a, b] = now[a] / (now[b] * (nodes[a] - nodes[b]))
    diff[0, 0], diff[7, 7] = -14.0, 14.0
    return diff.astype(np.float32), weights.astype(np.float32)


def table(rows_y):
    d, w = gll_tables()
    lane = np.arange(128)
    by_y, by_x = lane % 8, lane // rows_y % 8
    parts = [m[:, by_y] for m in (d, d.T, d * d, (d * d).T)]
    parts += [m[:, by_x] for m in (d, d.T, (d * d).T)]
    quad = (w[:, None, None] * np.tile(w, rows_y // 8)[None, :, None]) * np.tile(w, 16)
    return np.concatenate(parts + [quad.reshape(8 * rows_y, 128)], 0).astype(np.float32)


def split(v):
    hi = v.astype(BF16)
    return hi, (v - hi.astype(F32)).astype(BF16)


def dot(a, b):
    return jnp.dot(a, b, preferred_element_type=F32)


def left3(m, parts):
    hi, lo = parts
    return dot(m[...], jnp.concatenate([hi, lo, hi], 0))


def right3(parts, m):
    hi, lo = parts
    return dot(jnp.concatenate([hi, lo, hi], 1), m[...])


def sum_z(tiles):
    n = len(tiles)
    lane = lax.broadcasted_iota(jnp.int32, tiles[0].shape, 1)
    ups = [pltpu.roll(w, 127, 1) for w in tiles]
    downs = [pltpu.roll(w, 1, 1) for w in tiles]
    out = []
    for t, w in enumerate(tiles):
        zero = jnp.zeros_like(w)
        up = jnp.where(lane == 127, ups[t + 1] if t + 1 < n else zero, ups[t])
        down = jnp.where(lane == 0, downs[t - 1] if t > 0 else zero, downs[t])
        out.append(w + jnp.where((lane & 7) == 7, up, jnp.where((lane & 7) == 0, down, zero)))
    return out


def sum_rows(face):
    row = lax.broadcasted_iota(jnp.int32, face.shape, 0)
    up, down = pltpu.roll(face, 15, 0), pltpu.roll(face, 1, 0)
    zero = jnp.zeros_like(face)
    return face + jnp.where(row == 7, up, jnp.where(row == 8, down, zero))


def kernel(
    nx,
    ny,
    load_h,
    cond_h,
    flag_h,
    region,
    kappa,
    tab,
    sol_o,
    res_o,
    dir_o,
    fwd,
    back,
    zfwd,
    zback,
    dxy,
    dz,
    cond,
    flag,
    wbuf,
    wbuf2,
    coef,
    reac,
    keep,
    dinv,
    dface,
    mrow,
    rvec,
    uvec,
    vec,
    r0,
    z0,
    sx,
    sy,
    sc,
    rx,
    ry,
    rc,
    part,
    part2,
    arx,
    ary,
    in_sem,
    send_sem,
    recv_sem,
    ax_send,
    ax_recv,
    ay_send,
    ay_recv,
    out_sem,
):
    mx, my = lax.axis_index("gx"), lax.axis_index("gy")
    rows = 256
    nt = wbuf.shape[0]

    copies = [
        pltpu.make_async_copy(
            load_h.at[:, pl.ds(128 * t, 128)], wbuf.at[t], in_sem.at[t]
        )
        for t in range(nt)
    ]
    copies.append(pltpu.make_async_copy(cond_h, cond, in_sem.at[nt]))
    copies.append(pltpu.make_async_copy(flag_h.at[:, pl.ds(0, 128)], flag, in_sem.at[nt + 1]))
    for c in copies:
        c.start()

    rx[...] = jnp.zeros_like(rx)
    ry[...] = jnp.zeros_like(ry)
    rc[...] = jnp.zeros_like(rc)

    def inside(dx, dy):
        ok = None
        for d, m, n in ((dx, mx, nx), (dy, my, ny)):
            if d:
                c = m > 0 if d < 0 else m < n - 1
                ok = c if ok is None else jnp.logical_and(ok, c)
        return ok

    barrier = pltpu.get_barrier_semaphore()
    for d in range(1, nx):
        pl.semaphore_signal(
            barrier, inc=1, device_id=((mx + d) % nx, my), device_id_type=MESH
        )
    for d in range(1, ny):
        pl.semaphore_signal(
            barrier, inc=1, device_id=(mx, (my + d) % ny), device_id_type=MESH
        )
    for dx, dy in DIRS[4:]:

        @pl.when(inside(dx, dy))
        def _():
            pl.semaphore_signal(
                barrier, inc=1, device_id=(mx + dx, my + dy), device_id_type=MESH
            )

    rr = lax.broadcasted_iota(jnp.int32, (rows, rows), 0)
    cc = lax.broadcasted_iota(jnp.int32, (rows, rows), 1)
    on_y = (rr >> 3) == (cc >> 3)
    on_x = ((rr & 15) == (cc & 15)) & ((rr >> 7) == (cc >> 7))

    def y_matrix(n):
        p = jnp.concatenate([tab[8 * n : 8 * n + 8, :]] * (rows // 8), 0)
        return jnp.where(on_y, jnp.concatenate([p, p], 1), 0.0)

    def x_matrix(n):
        p = [jnp.broadcast_to(tab[8 * n + a : 8 * n + a + 1, :], (16, 128)) for a in range(8)]
        p = jnp.concatenate(p + p, 0)
        return jnp.where(on_x, jnp.concatenate([p, p], 1), 0.0)

    hi, lo = split(x_matrix(6) + y_matrix(3))
    for n, m in enumerate((hi, hi, lo)):
        dxy[:, rows * n : rows * (n + 1)] = m
    hi, lo = split(y_matrix(2))
    for n, m in enumerate((hi, hi, lo)):
        dz[rows * n : rows * (n + 1), :] = m
    hi, lo = split(y_matrix(0))
    for n, m in enumerate((hi, hi, lo)):
        fwd[rows:, rows * n : rows * (n + 1)] = m
        zback[rows * n : rows * (n + 1), :] = m
    hi, lo = split(y_matrix(1))
    for n, m in enumerate((hi, hi, lo)):
        back[:, rows * (2 * n + 1) : rows * (2 * n + 2)] = m
        zfwd[rows * n : rows * (n + 1), :] = m
    hi, lo = split(x_matrix(4))
    for n, m in enumerate((hi, hi, lo)):
        fwd[:rows, rows * n : rows * (n + 1)] = m
    hi, lo = split(x_matrix(5))
    for n, m in enumerate((hi, hi, lo)):
        back[:, rows * 2 * n : rows * (2 * n + 1)] = m

    ids = jnp.concatenate(
        [
            jnp.broadcast_to(region[ex, ey : ey + 1, :], (8, region.shape[2]))
            for ex in range(2)
            for ey in range(2)
        ],
        0,
    )
    kap = jnp.zeros(ids.shape, F32)
    for n in range(NREG):
        kap = jnp.where(ids == n, kappa[n], kap)
    k_hi, k_rest = kap.astype(BF16), kap - kap.astype(BF16).astype(F32)
    k_mid, k_lo = split(k_rest)
    el = lax.broadcasted_iota(jnp.int32, (ids.shape[1], 128 * nt), 0)
    at = lax.broadcasted_iota(jnp.int32, (ids.shape[1], 128 * nt), 1) >> 3
    spread = jnp.where(el == at, 1.0, 0.0).astype(BF16)
    kz = dot(k_hi, spread) + dot(k_mid, spread) + dot(k_lo, spread)
    q0 = tab[56:, :]
    quad = jnp.concatenate([q0, q0], 0)

    peers = jnp.int32(nx - 1 + ny - 1)
    for dx, dy in DIRS[4:]:
        peers = peers + inside(dx, dy).astype(jnp.int32)
    pl.semaphore_wait(barrier, peers)

    def ends(k, i, c):
        part = pl.ds(2 * c, 2)
        if i < 2:
            return sx.at[k, i, part], rx.at[k, OPP[i], part], rx.at[k, i, part]
        if i < 4:
            return sy.at[k, i - 2, part], ry.at[k, OPP[i] - 2, part], ry.at[k, i - 2, part]
        return sc.at[k, i - 4], rc.at[k, OPP[i] - 4], rc.at[k, i - 4]

    last = nt // 2 - 1

    def start(k, w, c):
        for t in (2 * c, 2 * c + 1):
            for side, row in ((0, 0), (1, rows - 16)):
                face = sum_rows(w[t, row : row + 16, :])
                sx[k, side, t] = face
                sc[k, 2 * side, t : t + 1, :] = face[0:1, :]
                sc[k, 2 * side + 1, t : t + 1, :] = face[15:16, :]
            for side, row in ((0, 0), (1, 15)):
                sy[k, side, t] = sum_rows(w[t, pl.ds(row, 16, stride=16), :])
        for i, (dx, dy) in enumerate(DIRS):
            if i >= 4 and c < last:
                continue

            @pl.when(inside(dx, dy))
            def _():
                src, dst, _ = ends(k, i, c)
                pltpu.make_async_remote_copy(
                    src_ref=src,
                    dst_ref=dst,
                    send_sem=send_sem.at[k, i, c],
                    recv_sem=recv_sem.at[k, OPP[i], c],
                    device_id=(mx + dx, my + dy),
                    device_id_type=MESH,
                ).start()

    def inner(w):
        for b in range(0, rows, 32):
            tiles = sum_z([w[t, b : b + 32, :] for t in range(nt)])
            for t in range(nt):
                w[t, b : b + 32, :] = tiles[t]
        for t in range(nt):
            s = w[t, 112:128, :] + w[t, 128:144, :]
            w[t, 112:128, :] = s
            w[t, 128:144, :] = s
            s = w[t, pl.ds(7, 16, stride=16), :] + w[t, pl.ds(8, 16, stride=16), :]
            w[t, pl.ds(7, 16, stride=16), :] = s
            w[t, pl.ds(8, 16, stride=16), :] = s

    def wait(k):
        for i, (dx, dy) in enumerate(DIRS):

            @pl.when(inside(dx, dy))
            def _():
                for c in range(last + 1):
                    if i >= 4 and c < last:
                        continue
                    src, _, dst = ends(k, i, c)
                    copy = pltpu.make_async_remote_copy(
                        src_ref=src,
                        dst_ref=dst,
                        send_sem=send_sem.at[k, i, c],
                        recv_sem=recv_sem.at[k, i, c],
                        device_id=(mx + dx, my + dy),
                        device_id_type=MESH,
                    )
                    copy.wait_recv()
                    copy.wait_send()

    def faces(t):
        return (
            (slice(0, 16), 0),
            (slice(rows - 16, rows), 1),
            (pl.ds(0, 16, stride=16), 2),
            (pl.ds(15, 16, stride=16), 3),
        )

    row16 = lax.broadcasted_iota(jnp.int32, (16, 128), 0)

    def raw(k, f, t):
        if f >= 2:
            return ry[k, f - 2, t]
        low, high = rc[k, 2 * f, t : t + 1, :], rc[k, 2 * f + 1, t : t + 1, :]
        zero = jnp.zeros((16, 128), F32)
        return rx[k, f, t] + jnp.where(row16 == 0, low, jnp.where(row16 == 15, high, zero))

    def arrived(k):
        return [sum_z([raw(k, f, t) for t in range(nt)]) for f in range(4)]

    def finish(k, w):
        wait(k)
        got = arrived(k)
        for t in range(nt):
            for where, f in faces(t):
                w[t, where, :] += got[f][t]

    def correct(k, scale, also=None):
        wait(k)
        got = arrived(k)
        for t in range(nt):
            for where, f in faces(t):
                h = got[f][t]
                vec[t, where, :] += (scale * dface[f, t]) * h
                if also is not None:
                    also[t, where, :] += keep[where, :] * h if t == 0 else h

    for c in copies[:nt]:
        c.wait()
    for c in range(nt // 2):
        start(0, wbuf, c)
    copies[nt].wait()
    copies[nt + 1].wait()
    for t in range(nt):
        coef[t] = quad * cond[:, 128 * t : 128 * (t + 1)].astype(F32)
        kt = kz[:, 128 * t : 128 * (t + 1)]
        kap = jnp.concatenate([kt[0:16]] * 8 + [kt[16:32]] * 8, 0)
        reac[t] = quad * kap
    lane = lax.broadcasted_iota(jnp.int32, (rows, 128), 1)
    keep[...] = jnp.where(lane == 0, (1 - flag[...]).astype(F32), 1.0)

    for c in range(nt // 2):
        cc = jnp.concatenate([coef[2 * c], coef[2 * c + 1]], 1)
        parts = split(cc)
        out = left3(dxy, parts) + right3(parts, dz)
        for h in range(2):
            t = 2 * c + h
            wbuf2[t] = out[:, 128 * h : 128 * (h + 1)] + reac[t]
        start(1, wbuf2, c)

    row = lax.broadcasted_iota(jnp.int32, (rows, 128), 0)
    px, py = mx * 16 + (row >> 4), my * 16 + (row & 15)
    share = jnp.ones((rows, 128), F32)
    for p, total in ((px, 16 * nx), (py, 16 * ny)):
        shared = ((p & 7) == 7) & (p != total - 1) | ((p & 7) == 0) & (p != 0)
        share = share * jnp.where(shared, 0.5, 1.0)
    mrow[...] = share
    part[...] = jnp.zeros_like(part)

    def lane_share(t):
        z = lax.broadcasted_iota(jnp.int32, (8, 128), 1) + 128 * t
        shared = ((z & 7) == 7) & (z != 128 * nt - 1) | ((z & 7) == 0) & (z != 0)
        return jnp.where(shared, 0.5, 1.0)

    def add_part(slot, t, prod):
        s = jnp.sum((prod * mrow[...]).reshape(rows // 8, 8, 128), axis=0)
        part[8 * slot : 8 * slot + 8, :] += s * lane_share(t)

    inner(wbuf)
    inner(wbuf2)
    finish(0, wbuf)
    finish(1, wbuf2)
    for t in range(nt):
        res, dia = wbuf[t], wbuf2[t]
        if t == 0:
            res = keep[...] * res
            dia = keep[...] * dia + (1.0 - keep[...])
        inv = 1.0 / dia
        r0[t] = res
        dinv[t] = inv
        vec[t] = res * inv * (1.0 / CENTER)
        for where, f in faces(t):
            inv = dinv[t, where, :]
            dface[f, t] = keep[where, :] * inv if t == 0 else inv

    def apply(k):
        for c in range(nt // 2):
            first = vec[2 * c]
            if c == 0:
                first = keep[...] * first
            v = jnp.concatenate([first, vec[2 * c + 1]], 1)
            cc = jnp.concatenate([coef[2 * c], coef[2 * c + 1]], 1)
            rr = jnp.concatenate([reac[2 * c], reac[2 * c + 1]], 1)
            parts = split(v)
            gxy = left3(fwd, parts)
            gz = right3(parts, zfwd)
            fxy = split(gxy * jnp.concatenate([cc, cc], 0))
            fz = split(gz * cc)
            out = left3(back, fxy) + right3(fz, zback) + rr * v
            wbuf[2 * c] = out[:, :128]
            wbuf[2 * c + 1] = out[:, 128:]
            start(k, wbuf, c)
        inner(wbuf)

    def image_of(t):
        out = wbuf[t]
        if t == 0:
            out = keep[...] * out + (1.0 - keep[...]) * vec[t]
        return out

    def reduce_copy(src, dst, sems, slot, dev):
        return pltpu.make_async_remote_copy(
            src_ref=src,
            dst_ref=dst,
            send_sem=sems[0].at[slot[0]],
            recv_sem=sems[1].at[slot[1]],
            device_id=dev,
            device_id_type=MESH,
        )

    k1 = 1.0 + C1 + CENTER * E1
    k2, k3 = 1.0 + C2, CENTER * E2 - C2
    apply(2)
    for t in range(nt):
        a0 = vec[t]
        new = k1 * a0 - (E1 * dinv[t]) * image_of(t)
        uvec[t] = a0
        vec[t] = new
    correct(2, -E1)
    apply(3)
    for t in range(nt):
        vec[t] = k2 * vec[t] + k3 * uvec[t] - (E2 * dinv[t]) * image_of(t)
    correct(3, -E2)
    apply(4)
    for t in range(nt):
        z, im = vec[t], image_of(t)
        z0[t] = z
        rvec[t] = im
        vec[t] = im * dinv[t] * (1.0 / CENTER)
        add_part(0, t, r0[t] * z)
    correct(4, 1.0 / CENTER, rvec)
    apply(5)
    for t in range(nt):
        add_part(1, t, rvec[t] * z0[t])
    finish(5, wbuf)
    for t in range(nt):
        a0, im, az = vec[t], rvec[t], image_of(t)
        a1 = k1 * a0 - (E1 * dinv[t]) * az
        uvec[t] = a0
        vec[t] = a1
        add_part(2, t, im * (k2 * a1 + k3 * a0) - (CENTER * E2) * (az * a1))
    arx[mx] = part[...]
    for d in range(1, nx):
        to = (mx + d) % nx
        reduce_copy(part, arx.at[mx], (ax_send, ax_recv), (d, mx), (to, my)).start()
    apply(6)
    for d in range(1, nx):
        frm = (mx + nx - d) % nx
        c = reduce_copy(part, arx.at[frm], (ax_send, ax_recv), (d, frm), (frm, my))
        c.wait_recv()
        c.wait_send()
    total = arx[0]
    for d in range(1, nx):
        total = total + arx[d]
    part2[...] = total
    ary[my] = total
    for d in range(1, ny):
        to = (my + d) % ny
        reduce_copy(part2, ary.at[my], (ay_send, ay_recv), (d, my), (mx, to)).start()
    for t in range(nt):
        vec[t] = k2 * vec[t] + k3 * uvec[t] - (E2 * dinv[t]) * image_of(t)
    correct(6, -E2)
    for d in range(1, ny):
        frm = (my + ny - d) % ny
        c = reduce_copy(part2, ary.at[frm], (ay_send, ay_recv), (d, frm), (mx, frm))
        c.wait_recv()
        c.wait_send()
    total = ary[0]
    for d in range(1, ny):
        total = total + ary[d]

    def whole(slot):
        return jnp.sum(total[8 * slot : 8 * slot + 8], axis=(0, 1), keepdims=True)

    first, curv, quadratic = whole(0), whole(1), whole(2)
    step = first / curv
    second = step * step * quadratic - first
    beta1 = 1.0 + second / first
    stores = []
    for t in range(nt):
        wbuf[t] = step * z0[t]
        wbuf2[t] = r0[t] - step * rvec[t]
        vec[t] = beta1 * z0[t] - step * vec[t]
        for n, (src, dst) in enumerate(((wbuf, sol_o), (wbuf2, res_o), (vec, dir_o))):
            c = pltpu.make_async_copy(
                src.at[t], dst.at[:, pl.ds(128 * t, 128)], out_sem.at[n, t]
            )
            c.start()
            stores.append(c)
    for c in stores:
        c.wait()


def store_kernel(a, b, c, oa, ob, oc, buf, in_sem, out_sem):
    rows = a.shape[0] // 2
    ins, outs = [], []
    for n, (src, dst) in enumerate(((a, oa), (b, ob), (c, oc))):
        for h in range(2):
            part = pl.ds(rows * h, rows)
            ins.append(
                pltpu.make_async_copy(src.at[part, :], buf.at[n, h], in_sem.at[n, h])
            )
            outs.append(
                pltpu.make_async_copy(buf.at[n, h], dst.at[part, :], out_sem.at[n, h])
            )
    for copy in ins:
        copy.start()
    for copy, out in zip(ins, outs):
        copy.wait()
        out.start()
    for out in outs:
        out.wait()


def per_device(nx, ny, load, conductivity, flags, region, kappa_table):
    rows_x, rows_y, rows_z = load.shape
    rows, nt = rows_x * rows_y, rows_z // 128
    big = pltpu.VMEM((nt, rows, 128), F32)
    face = pltpu.VMEM((ROUNDS, 2, nt, 16, 128), F32)
    line = pltpu.VMEM((ROUNDS, 4, 8, 128), F32)
    vm = pl.BlockSpec(memory_space=pltpu.VMEM)
    hbm = pl.BlockSpec(memory_space=pltpu.HBM)
    out = jax.ShapeDtypeStruct((rows, rows_z), F32)
    dma = pltpu.SemaphoreType.DMA
    outs = pl.pallas_call(
        functools.partial(kernel, nx, ny),
        out_shape=(out, out, out),
        in_specs=[hbm] * 3 + [vm, pl.BlockSpec(memory_space=pltpu.SMEM), vm],
        out_specs=(hbm, hbm, hbm),
        scratch_shapes=[
            pltpu.VMEM((2 * rows, 3 * rows), BF16),
            pltpu.VMEM((rows, 6 * rows), BF16),
            pltpu.VMEM((3 * rows, rows), BF16),
            pltpu.VMEM((3 * rows, rows), BF16),
            pltpu.VMEM((rows, 3 * rows), BF16),
            pltpu.VMEM((3 * rows, rows), BF16),
            pltpu.VMEM((rows, rows_z), BF16),
            pltpu.VMEM((rows, 128), jnp.int32),
            big,
            big,
            big,
            big,
            pltpu.VMEM((rows, 128), F32),
            big,
            pltpu.VMEM((4, nt, 16, 128), F32),
            pltpu.VMEM((rows, 128), F32),
            big,
            big,
            big,
            big,
            big,
            face,
            face,
            line,
            face,
            face,
            line,
            pltpu.VMEM((24, 128), F32),
            pltpu.VMEM((24, 128), F32),
            pltpu.VMEM((nx, 24, 128), F32),
            pltpu.VMEM((ny, 24, 128), F32),
            dma((nt + 2,)),
            dma((ROUNDS, 8, nt // 2)),
            dma((ROUNDS, 8, nt // 2)),
            dma((nx,)),
            dma((nx,)),
            dma((ny,)),
            dma((ny,)),
            dma((3, nt)),
        ],
        compiler_params=pltpu.CompilerParams(
            collective_id=0, has_side_effects=True, vmem_limit_bytes=62 << 20
        ),
    )(
        load.reshape(rows, rows_z),
        conductivity.reshape(rows, rows_z),
        flags.reshape(rows, rows_z),
        region,
        kappa_table,
        jnp.asarray(table(rows_y)),
    )
    outs = pl.pallas_call(
        store_kernel,
        out_shape=(out, out, out),
        in_specs=[hbm] * 3,
        out_specs=(hbm, hbm, hbm),
        scratch_shapes=[
            pltpu.VMEM((3, 2, rows // 2, rows_z), F32),
            dma((3, 2)),
            dma((3, 2)),
        ],
        compiler_params=pltpu.CompilerParams(vmem_limit_bytes=62 << 20),
    )(*outs)
    return tuple(o.reshape(load.shape) for o in outs)


def solution(mesh):
    cut = P("gx", "gy", None)
    return jax.shard_map(
        functools.partial(per_device, mesh.shape["gx"], mesh.shape["gy"]),
        mesh=mesh,
        in_specs=(cut, cut, cut, cut, P()),
        out_specs=(cut, cut, cut),
        check_vma=False,
    )
```
